1024 devices in a mesh: gx: 64 (over y, z), gy: 16 (over x, core).
Axes of the slice: x: 8, y: 8, z: 8, core: 2. Of those that a mesh axis runs over, the one named last changes fastest.
Arguments:
- old_boxes: float32 [64, 16, 16, 5, 512], P('gx', 'gy'), may hold values from -1 to 5.75, as said below
- send_slot: int32 [64, 16, 16, 2], P('gx', 'gy'), may hold values from 0 to 16, as said below
- arrival: int32 [64, 16, 8], P('gx', 'gy'), may hold values from 0 to 31, as said below
- coarse: float32 [64, 16, 5, 800], P('gx', 'gy'), may hold values from -1 to 5.75, as said below
- coarse_flux: float32 [64, 16, 5, 256], P('gx', 'gy'), may hold values from -6 to 6
Outputs:
- fine_out: float32 [64, 16, 8, 5, 512], P('gx', 'gy')
- coarse_out: float32 [64, 16, 5, 800], P('gx', 'gy')
The draws below stay inside these ranges and needn't reach their ends.
Inputs may be any that keep to these rules, and one draw needn't show every extreme that they name: Within each segment, send_slot[g, s, d, c] is the old slot of source s holding the c-th box that s sends to d, or 16 where s sends nothing to d; a pair carries 2 boxes or none; no old slot is sent twice; every destination receives exactly 8 boxes; old slots never named hold no box. arrival[g, d, k] = s * 2 + c names the c-th box that s sends to d, which becomes box k of d; every box sent to d is named once. `old_boxes`: every slot holds the conserved fields of a state with density and pressure in [0.5, 2] and velocity components in [-0.5, 0.5]. `coarse`: every cell holds the conserved fields of a state with density and pressure in [0.5, 2] and velocity components in [-0.5, 0.5].
All inputs are finite; a program needn't handle non-finite values.
Results may differ from the reference program's by a relative error of at most 0.0003.
Values sent between devices are 32-bit elements; how exact they have to be, the bound alone decides.
No kernel may reach another device: no remote copies, remote signals or barrier semaphores. Data moves between devices by JAX's collectives and lax.ppermute only.
A program may use at most 32 MiB of HBM per device.

```python
import jax
import jax.numpy as jnp
from jax import lax

NF = 5
BXY = 16
BZ = 2
CAP = 2
BOX_DEV = 8
OLD_SLOTS = 16
CELLS = 512
CZ = 8
CYCLE = 100
N_GX = 64
N_GY = 16


GAMMA = 1.4


def segment_plan(key):
    groups = N_GX
    peers = N_GY
    pair_count = BOX_DEV // CAP
    key_shuffle = jax.random.fold_in(key, 101)
    key_slots = jax.random.fold_in(key, 202)
    shuffled = jax.vmap(lambda sub: jax.random.permutation(sub, peers))(jax.random.split(key_shuffle, groups)).astype(jnp.int32)
    receiver = jnp.arange(peers, dtype=jnp.int32)[:, None]
    pair_turn = jnp.arange(pair_count, dtype=jnp.int32)[None, :]
    position = receiver + pair_turn * peers
    heavy_span = peers // 4 * 2 * pair_count
    rank_index = jnp.where(position < heavy_span, position // (2 * pair_count), peers // 4 + (position - heavy_span) // pair_count)
    run_index = jnp.where(position < heavy_span, position % (2 * pair_count), (position - heavy_span) % pair_count)
    source = shuffled[:, rank_index]
    slot_order = jax.vmap(lambda sub: jax.random.permutation(sub, OLD_SLOTS))(jax.random.split(key_slots, groups * peers))
    slot_order = slot_order.astype(jnp.int32).reshape(groups, peers, OLD_SLOTS)
    lane_index = jnp.arange(CAP, dtype=jnp.int32)[None, None, None, :]
    group_index = jnp.arange(groups, dtype=jnp.int32)[:, None, None, None]
    sender = jnp.broadcast_to(source[:, :, :, None], (groups, peers, pair_count, CAP))
    slot_pick = run_index[None, :, :, None] * CAP + lane_index
    old_slot = slot_order[group_index, sender, slot_pick]
    target = jnp.broadcast_to(jnp.arange(peers, dtype=jnp.int32)[None, :, None, None], sender.shape)
    send_table = jnp.full((groups, peers, peers, CAP), OLD_SLOTS, dtype=jnp.int32)
    send_table = send_table.at[jnp.broadcast_to(group_index, sender.shape), sender, target, jnp.broadcast_to(lane_index, sender.shape)].set(old_slot)
    arrive = (sender * CAP + lane_index).reshape(groups, peers, BOX_DEV)
    return (send_table, arrive.astype(jnp.int32))


def flow_state(key, lead_shape, stack_axis, exponent, tail_power):
    subkeys = jax.random.split(key, 3)
    density = 0.5 * 4.0 ** jax.random.uniform(subkeys[0], lead_shape, dtype=jnp.float32) ** exponent
    pressure = 0.5 * 4.0 ** jax.random.uniform(subkeys[1], lead_shape, dtype=jnp.float32) ** exponent
    swing_draw = jax.random.uniform(subkeys[2], (3,) + lead_shape, dtype=jnp.float32, minval=-1.0, maxval=1.0)
    velocity = 0.5 * jnp.sign(swing_draw) * jnp.abs(swing_draw) ** tail_power
    energy = pressure / (GAMMA - 1.0) + 0.5 * density * jnp.sum(velocity * velocity, axis=0)
    fields = [density, density * velocity[0], density * velocity[1], density * velocity[2], energy]
    return jnp.stack(fields, axis=stack_axis)


def draw_send_slot(key, part):
    plan = segment_plan(key)
    return plan[0]


def draw_arrival(key, part):
    plan = segment_plan(key)
    return plan[1]


def draw_old_boxes(key, part):
    key = jax.random.fold_in(key, 3)
    lead_shape = (N_GX, N_GY, OLD_SLOTS, CELLS)
    return flow_state(key, lead_shape, 3, 1.0, 1.0)


def draw_coarse(key, part):
    key = jax.random.fold_in(key, 7)
    lead_shape = (N_GX, N_GY, CZ * CYCLE)
    return flow_state(key, lead_shape, 2, 1.0, 1.0)


def block_scale(own_key, shape, cuts, low, top_value):
    def one(dim, blocks):
        heights = jax.random.uniform(jax.random.fold_in(jax.random.fold_in(own_key, 6), dim), (blocks,), jnp.float32, low / len(cuts), top_value / len(cuts))
        return jnp.repeat(jnp.exp(heights), shape[dim] // blocks).reshape((-1,) + (1,) * (len(shape) - dim - 1))

    factor_of = one(*cuts[0])
    for cut in cuts[1:]:
        factor_of = factor_of * one(*cut)
    return factor_of


def normal_values(own_key, extent, scale, limit, shards=(), kind=jnp.bfloat16):
    loudness = block_scale(own_key, extent, shards, -0.22, 0.18) if shards else 1.0
    result = jax.random.normal(own_key, extent, jnp.float32) * scale * loudness
    return jnp.minimum(jnp.maximum(result, -limit), limit).astype(kind)


def setup_inputs(seed: int = 0) -> dict:
    key_list = jax.random.split(jax.random.key(seed), 6)
    old_boxes = draw_old_boxes(jax.random.fold_in(key_list[5], 71), 0)
    send_slot = draw_send_slot(jax.random.fold_in(key_list[5], 71), 0)
    arrival = draw_arrival(jax.random.fold_in(key_list[5], 71), 0)
    coarse = draw_coarse(jax.random.fold_in(key_list[5], 71), 0)
    coarse_flux = normal_values(key_list[4], (N_GX, N_GY, NF, CZ * 2 * BXY), 1.0, 6.0, ((0, 64), (1, 16)), jnp.float32)
    return {"old_boxes": old_boxes, "send_slot": send_slot, "arrival": arrival, "coarse": coarse, "coarse_flux": coarse_flux}


GAMMA = 1.4
STEP_RATIO = 0.1

def primitive(fields):
    density = fields[0]
    velocity = fields[1:4] / density
    pressure = (GAMMA - 1.0) * (fields[4] - 0.5 * density * lax.optimization_barrier(jnp.sum(velocity * velocity, axis=0)))
    return jnp.concatenate([density[None], velocity, pressure[None]], axis=0)

def minmod(first_delta, second_delta):
    return 0.5 * (jnp.sign(first_delta) + jnp.sign(second_delta)) * jnp.minimum(jnp.abs(first_delta), jnp.abs(second_delta))

def conserved_flux(primitives, component):
    density = primitives[0]
    velocity = primitives[1:4]
    pressure = primitives[4]
    normal = velocity[component - 1]
    energy = pressure / (GAMMA - 1.0) + 0.5 * density * lax.optimization_barrier(jnp.sum(velocity * velocity, axis=0))
    conserved = jnp.concatenate([density[None], density * velocity, energy[None]], axis=0)
    momentum_flux = density * normal * velocity
    momentum_flux = momentum_flux.at[component - 1].add(pressure)
    flux_all = jnp.concatenate([(density * normal)[None], momentum_flux, ((energy + pressure) * normal)[None]], axis=0)
    wave_speed = jnp.abs(normal) + jnp.sqrt(GAMMA * pressure / density)
    return (conserved, flux_all, wave_speed)

def face_flux(padded, axis_index, component):
    length = padded.shape[axis_index]
    interior = length - 4
    deltas = lax.slice_in_dim(padded, 1, length, axis=axis_index) - lax.slice_in_dim(padded, 0, length - 1, axis=axis_index)
    slopes = minmod(lax.slice_in_dim(deltas, 0, length - 2, axis=axis_index), lax.slice_in_dim(deltas, 1, length - 1, axis=axis_index))
    lower_state = lax.slice_in_dim(padded, 1, interior + 2, axis=axis_index) + 0.5 * lax.slice_in_dim(slopes, 0, interior + 1, axis=axis_index)
    upper_state = lax.slice_in_dim(padded, 2, interior + 3, axis=axis_index) - 0.5 * lax.slice_in_dim(slopes, 1, interior + 2, axis=axis_index)
    cons_lower, flux_lower, speed_lower = conserved_flux(lower_state, component)
    cons_upper, flux_upper, speed_upper = conserved_flux(upper_state, component)
    return 0.5 * (flux_lower + flux_upper) - 0.5 * jnp.maximum(speed_lower, speed_upper) * (cons_upper - cons_lower)

def cycle_faces(coarse_block):
    return jnp.stack([coarse_block[:, :, 1:-1, 0], coarse_block[:, :, 1:-1, -1], coarse_block[:, :, 0, 1:-1], coarse_block[:, :, -1, 1:-1]], axis=2)

def expand(coarse_faces):
    widened = jnp.repeat(jnp.repeat(coarse_faces, 2, axis=1), 2, axis=3)
    return jnp.broadcast_to(widened[:, :, :, None, :], widened.shape[:3] + (2, widened.shape[3]))

def advance(fields, lower_rim, upper_rim, ghosts_all):
    primitives = primitive(fields)
    prim_z = jnp.concatenate([primitive(lower_rim), primitives, primitive(upper_rim)], axis=1)
    ghost_prim = primitive(ghosts_all)
    prim_y = jnp.concatenate([ghost_prim[:, :, 2], primitives, ghost_prim[:, :, 3]], axis=2)
    prim_x = jnp.concatenate([jnp.swapaxes(ghost_prim[:, :, 0], 2, 3), primitives, jnp.swapaxes(ghost_prim[:, :, 1], 2, 3)], axis=3)
    flux_z = face_flux(prim_z, 1, 3)
    flux_y = face_flux(prim_y, 2, 2)
    flux_x = face_flux(prim_x, 3, 1)
    change = flux_z[:, 1:] - flux_z[:, :-1] + (flux_y[:, :, 1:] - flux_y[:, :, :-1]) + (flux_x[..., 1:] - flux_x[..., :-1])
    new_fields = fields - STEP_RATIO * change
    side_flux = jnp.stack([flux_x[..., 0], flux_x[..., -1], flux_y[:, :, 0, :], flux_y[:, :, -1, :]], axis=2)
    return (new_fields, side_flux)

def restrict(new_fields, side_flux):
    layers = new_fields.shape[1] // 2
    half_edge = BXY // 2
    face_mean = side_flux.reshape(NF, layers, 2, 4, half_edge, 2).mean(axis=(2, 5))
    averaged = new_fields.reshape(NF, layers, 2, half_edge, 2, half_edge, 2).mean(axis=(2, 4, 6))
    return (face_mean, averaged)

def coarse_update(coarse_block, face_mean, averaged, register):
    signs = jnp.array([-1.0, 1.0, -1.0, 1.0], dtype=coarse_block.dtype)
    correction = 0.5 * STEP_RATIO * (face_mean - register) * signs[None, None, :, None]
    new_block = coarse_block.at[:, :, 1:-1, 1:-1].set(averaged)
    new_block = new_block.at[:, :, 1:-1, 0].add(correction[:, :, 0])
    new_block = new_block.at[:, :, 1:-1, -1].add(correction[:, :, 1])
    new_block = new_block.at[:, :, 0, 1:-1].add(correction[:, :, 2])
    new_block = new_block.at[:, :, -1, 1:-1].add(correction[:, :, 3])
    return new_block

def to_column(new_boxes):
    box_count = new_boxes.shape[0]
    return new_boxes.reshape(box_count, NF, BZ, BXY, BXY).transpose(1, 0, 2, 3, 4).reshape(NF, box_count * BZ, BXY, BXY)

def from_column(new_fields):
    box_count = new_fields.shape[1] // BZ
    return new_fields.reshape(NF, box_count, BZ * BXY * BXY).transpose(1, 0, 2)

def reference(old_boxes, send_slot, arrival, coarse, coarse_flux):
    groups = old_boxes.shape[0]
    peers = old_boxes.shape[1]
    half_axis = groups // 2
    coarse_column = jnp.roll(coarse, half_axis, axis=0)
    flux_column = jnp.roll(coarse_flux, half_axis, axis=0)
    edge = BXY // 2 + 2

    def one_group(pieces):
        old_group, send_group, arrive, blocks, registers = pieces
        capacity = send_group.shape[2]
        source = arrive // capacity
        lane_index = arrive % capacity
        receiver = jnp.arange(peers, dtype=jnp.int32)[:, None]
        old_slot = send_group[source, receiver, lane_index]
        new_boxes = old_group[source, old_slot]
        per_device = new_boxes.shape[1]
        fields = to_column(new_boxes.reshape(peers * per_device, NF, -1))
        coarse_block = blocks.reshape(peers, NF, -1, edge, edge).transpose(1, 0, 2, 3, 4).reshape(NF, -1, edge, edge)
        register = registers.reshape(peers, NF, -1, 4, BXY // 2).transpose(1, 0, 2, 3, 4).reshape(NF, -1, 4, BXY // 2)
        ghosts_all = expand(cycle_faces(coarse_block))
        new_fields, side_flux = advance(fields, fields[:, -2:], fields[:, :2], ghosts_all)
        face_mean, averaged = restrict(new_fields, side_flux)
        new_block = coarse_update(coarse_block, face_mean, averaged, register)
        fine_boxes = from_column(new_fields).reshape(peers, per_device, NF, -1)
        coarse_back = new_block.reshape(NF, peers, -1, edge, edge).transpose(1, 0, 2, 3, 4).reshape(peers, NF, -1)
        return (fine_boxes, coarse_back)
    fine_out, coarse_new = lax.map(one_group, (old_boxes, send_slot, arrival, coarse_column, flux_column))
    return (fine_out, jnp.roll(coarse_new, half_axis, axis=0))
```

```python
import jax
import jax.numpy as jnp
import numpy as np
from jax import lax
from jax.experimental import pallas as pl
from jax.experimental.pallas import tpu as pltpu
from jax.sharding import PartitionSpec as P

NF = 5
BXY = 16
EDGE = BXY // 2 + 2
CYCLE = EDGE * EDGE
LANES = 128
ROWS = 20
STEP_RATIO = 0.1
HIGHEST = lax.Precision.HIGHEST


def lane_iota():
    return lax.broadcasted_iota(jnp.int32, (8, LANES), 1)


def selection_matrices():
    ghost = np.zeros((LANES, 3 * LANES), np.float32)
    mean = np.zeros((5 * LANES, LANES), np.float32)
    for y in range(BXY):
        for x in range(BXY):
            lane = y * BXY + x
            cy, cx = (1 + y // 2, 1 + x // 2)
            mean[lane, cy * EDGE + cx] = 1.0 / 8.0
            if x == 0:
                ghost[cy * EDGE, lane] = 1.0
                mean[2 * LANES + lane, cy * EDGE] = -0.25
            if x == BXY - 1:
                ghost[cy * EDGE + EDGE - 1, lane] = 1.0
                mean[2 * LANES + lane, cy * EDGE + EDGE - 1] = 0.25
            if y == 0:
                ghost[cx, 2 * LANES + x] = 1.0
                mean[4 * LANES + x, cx] = -0.25
            if y == BXY - 1:
                ghost[(EDGE - 1) * EDGE + cx, 2 * LANES + LANES - BXY + x] = 1.0
                mean[4 * LANES + LANES - BXY + x, (EDGE - 1) * EDGE + cx] = 0.25
    register = np.zeros((LANES, LANES), np.float32)
    for t in range(BXY // 2):
        register[t, (1 + t) * EDGE] = 1.0
        register[8 + t, (1 + t) * EDGE + EDGE - 1] = -1.0
        register[16 + t, 1 + t] = 1.0
        register[24 + t, (EDGE - 1) * EDGE + 1 + t] = -1.0
    return (ghost, mean, register)


def minmod(a, b):
    return jnp.maximum(jnp.minimum(a, b), 0.0) + jnp.minimum(jnp.maximum(a, b), 0.0)


def primitive(u):
    inverse = 1.0 / u[0]
    v = [u[i] * inverse for i in (1, 2, 3)]
    pressure = 0.4 * (u[4] - 0.5 * u[0] * (v[0] * v[0] + v[1] * v[1] + v[2] * v[2]))
    return [u[0]] + v + [pressure]


def state_terms(q, normal):
    density, velocity, pressure = (q[0], q[1:4], q[4])
    kinetic = velocity[0] * velocity[0] + velocity[1] * velocity[1] + velocity[2] * velocity[2]
    energy = 2.5 * pressure + 0.5 * density * kinetic
    momentum = [density * v for v in velocity]
    vn = velocity[normal]
    mass = momentum[normal]
    flux = [mass] + [mass * v for v in velocity] + [(energy + pressure) * vn]
    flux[1 + normal] = flux[1 + normal] + pressure
    scaled = 1.4 * pressure
    speed = jnp.abs(vn) + scaled * lax.rsqrt(scaled * density)
    return ([density] + momentum + [energy], flux, speed)


def face_flux(lower, upper, normal):
    cons_l, flux_l, speed_l = state_terms(lower, normal)
    cons_u, flux_u, speed_u = state_terms(upper, normal)
    half = 0.5 * jnp.maximum(speed_l, speed_u)
    return [
        0.5 * (fl + fu) - half * (cu - cl) for fl, fu, cl, cu in zip(flux_l, flux_u, cons_l, cons_u)
    ]


def lane_roll(value, shift):
    return pltpu.roll(value, shift % LANES, 1)


def pack_kernel(slots_ref, boxes_ref, out_ref):
    def one(d, carry):
        first = slots_ref[0, d]

        @pl.when(first < boxes_ref.shape[1])
        def _():
            second = jnp.minimum(slots_ref[1, d], boxes_ref.shape[1] - 1)
            for c, slot in enumerate((first, second)):
                for f in range(NF):
                    box = boxes_ref[f, pl.ds(slot, 1), :]
                    for q in range(4):
                        out_ref[d, pl.ds(c * ROWS + f * 4 + q, 1), :] = box[:, q * LANES : (q + 1) * LANES]

        return carry

    lax.fori_loop(0, out_ref.shape[0], one, 0)


def ghost_kernel(coarse_ref, flux_ref, ghost_m_ref, register_m_ref, ghosts_ref, base_ref):
    lane = lane_iota()
    row = lax.broadcasted_iota(jnp.int32, (8, LANES), 0)
    on_block = lane < CYCLE
    cy, cx = (lane // EDGE, lane % EDGE)
    interior = (cy >= 1) & (cy <= EDGE - 2) & (cx >= 1) & (cx <= EDGE - 2)
    blocks = []
    registers = []
    for f in range(NF):
        tiles = [coarse_ref[f, :, pl.ds(t * LANES, LANES)] for t in range(6)]
        tiles.append(
            jnp.concatenate(
                [coarse_ref[f, :, pl.ds(6 * LANES, 8 * CYCLE - 6 * LANES)], jnp.zeros((1, 7 * LANES - 8 * CYCLE), jnp.float32)],
                axis=1,
            )
        )
        rows = []
        for l in range(8):
            start = l * CYCLE
            t, off = divmod(start, LANES)
            first = jnp.broadcast_to(tiles[t], (8, LANES))
            piece = lane_roll(first, -off)
            if off + CYCLE > LANES:
                second = lane_roll(jnp.broadcast_to(tiles[t + 1], (8, LANES)), -off)
                piece = jnp.where(lane < LANES - off, piece, second)
            rows.append(piece)
        block = rows[0]
        for l in range(1, 8):
            block = jnp.where(row == l, rows[l], block)
        blocks.append(block)
        reg = None
        for l in range(8):
            t, off = divmod(l * 32, LANES)
            piece = lane_roll(jnp.broadcast_to(flux_ref[f, :, pl.ds(t * LANES, LANES)], (8, LANES)), -off)
            reg = piece if reg is None else jnp.where(row == l, piece, reg)
        registers.append(reg)
    safe = [jnp.where(on_block, b, 1.0) for b in blocks]
    prims = jnp.concatenate(primitive(safe), axis=0)
    spread = jnp.dot(prims, ghost_m_ref[...], precision=HIGHEST, preferred_element_type=jnp.float32)
    placed = jnp.dot(
        jnp.concatenate(registers, axis=0), register_m_ref[...], precision=HIGHEST, preferred_element_type=jnp.float32
    )
    for f in range(NF):
        for t in range(3):
            ghosts_ref[f, t] = spread[f * 8 : f * 8 + 8, t * LANES : (t + 1) * LANES]
        kept = jnp.where(on_block & ~interior, blocks[f], 0.0)
        base_ref[f] = kept + (0.5 * STEP_RATIO) * placed[f * 8 : f * 8 + 8]


def side_kernel(arrive_ref, received_ref, ghosts_ref, base_ref, mean_ref, part_ref, prim_ref, coarse_ref, fields):
    def one(k, carry):
        start = arrive_ref[0, k] * ROWS
        for f in range(NF):
            for q in range(4):
                fields[f, q, pl.ds(k, 1), :] = received_ref[pl.ds(start + f * 4 + q, 1), :]
        return carry

    lax.fori_loop(0, 8, one, 0)
    lane = lane_iota()
    x = lane % BXY
    first_x, last_x = (x == 0, x == BXY - 1)
    low_y, high_y = (lane < BXY, lane >= LANES - BXY)
    cells = [[fields[f, q] for f in range(NF)] for q in range(4)]
    prims = [primitive(c) for c in cells]
    ghost = [[ghosts_ref[f, t] for f in range(NF)] for t in range(3)]
    change = []
    x_sides = [None, None]
    for q in range(4):
        h = q % 2
        g = ghost[h]
        lower, upper, top = ([], [], [])
        for f in range(NF):
            p = prims[q][f]
            below = jnp.where(first_x, g[f], lane_roll(p, 1))
            above = jnp.where(last_x, g[f], lane_roll(p, -1))
            half = 0.5 * minmod(p - below, above - p)
            high = p + half
            lower.append(jnp.where(first_x, g[f], lane_roll(high, 1)))
            upper.append(p - half)
            top.append((high, jnp.where(last_x, g[f], p)))
        low_flux = face_flux(lower, upper, 0)
        top_flux = face_flux([t[0] for t in top], [t[1] for t in top], 0)
        change.append(
            [jnp.where(last_x, t, lane_roll(l, -1)) - l for l, t in zip(low_flux, top_flux)]
        )
        side = [jnp.where(first_x, l, jnp.where(last_x, t, 0.0)) for l, t in zip(low_flux, top_flux)]
        x_sides[h] = side if x_sides[h] is None else [a + b for a, b in zip(x_sides[h], side)]
    y_sides = None
    for j in range(2):
        q0, q1 = (2 * j, 2 * j + 1)
        g = ghost[2]
        states = ([], [], [], [], [], [])
        for f in range(NF):
            p0, p1 = (prims[q0][f], prims[q1][f])
            up0, up1 = (lane_roll(p0, BXY), lane_roll(p1, BXY))
            down0, down1 = (lane_roll(p0, -BXY), lane_roll(p1, -BXY))
            below0, below1 = (jnp.where(low_y, g[f], up0), jnp.where(low_y, up0, up1))
            above0, above1 = (jnp.where(high_y, down1, down0), jnp.where(high_y, g[f], down1))
            half0 = 0.5 * minmod(p0 - below0, above0 - p0)
            half1 = 0.5 * minmod(p1 - below1, above1 - p1)
            high0, high1 = (p0 + half0, p1 + half1)
            roll0, roll1 = (lane_roll(high0, BXY), lane_roll(high1, BXY))
            for one_list, value in zip(
                states,
                (
                    jnp.where(low_y, g[f], roll0),
                    p0 - half0,
                    jnp.where(low_y, roll0, roll1),
                    p1 - half1,
                    high1,
                    jnp.where(high_y, g[f], p1),
                ),
            ):
                one_list.append(value)
        flux0 = face_flux(states[0], states[1], 1)
        flux1 = face_flux(states[2], states[3], 1)
        top = face_flux(states[4], states[5], 1)
        for f in range(NF):
            next0, next1 = (lane_roll(flux0[f], -BXY), lane_roll(flux1[f], -BXY))
            change[q0][f] = change[q0][f] + (jnp.where(high_y, next1, next0) - flux0[f])
            change[q1][f] = change[q1][f] + (jnp.where(high_y, top[f], next1) - flux1[f])
        side = [jnp.where(low_y, a, jnp.where(high_y, b, 0.0)) for a, b in zip(flux0, top)]
        y_sides = side if y_sides is None else [a + b for a, b in zip(y_sides, side)]
    parts = [[c - STEP_RATIO * d for c, d in zip(cells[q], change[q])] for q in range(4)]
    for f in range(NF):
        for q in range(4):
            part_ref[f, q] = parts[q][f]
            prim_ref[f, q] = prims[q][f]
    scale = 0.5 * STEP_RATIO
    stacked = jnp.concatenate(
        [
            jnp.concatenate([parts[0][f] + parts[2][f] for f in range(NF)], axis=0),
            jnp.concatenate([parts[1][f] + parts[3][f] for f in range(NF)], axis=0),
            jnp.concatenate([scale * x_sides[0][f] for f in range(NF)], axis=0),
            jnp.concatenate([scale * x_sides[1][f] for f in range(NF)], axis=0),
            jnp.concatenate([scale * y_sides[f] for f in range(NF)], axis=0),
        ],
        axis=1,
    )
    coarse = jnp.dot(stacked, mean_ref[...], precision=HIGHEST, preferred_element_type=jnp.float32)
    for f in range(NF):
        coarse_ref[f] = base_ref[f] + coarse[f * 8 : f * 8 + 8]


def column_kernel(before_ref, after_ref, part_ref, prim_ref, coarse_ref, mean_ref, fine_ref, out_ref):
    lane = lane_iota()
    row = lax.broadcasted_iota(jnp.int32, (8, LANES), 0)
    first, last = (row == 0, row == 7)

    def down(value, edge):
        return jnp.where(first, edge, pltpu.roll(value, 1, 0))

    def up(value, edge):
        return jnp.where(last, edge, pltpu.roll(value, 7, 0))

    before = [primitive([before_ref[f * 4 + q : f * 4 + q + 1, :] for f in range(NF)]) for q in range(4)]
    after = [primitive([after_ref[f * 4 + q : f * 4 + q + 1, :] for f in range(NF)]) for q in range(4)]
    sums = []
    for h in range(2):
        states = ([], [], [], [], [], [])
        for f in range(NF):
            p0, p1 = (prim_ref[f, h], prim_ref[f, 2 + h])
            b0, b1 = (before[h][f], before[2 + h][f])
            a0, a1 = (after[h][f], after[2 + h][f])
            step = p1 - p0
            half0 = 0.5 * minmod(p0 - down(p1, b1), step)
            half1 = 0.5 * minmod(step, up(p0, a0) - p1)
            half_b = 0.5 * minmod(b1 - b0, p0[0:1] - b1)
            half_a = 0.5 * minmod(a0 - p1[7:8], a1 - a0)
            high1 = p1 + half1
            for one_list, value in zip(
                states,
                (down(high1, b1 + half_b), p0 - half0, p0 + half0, p1 - half1, high1[7:8], a0 - half_a),
            ):
                one_list.append(value)
        flux0 = face_flux(states[0], states[1], 2)
        flux1 = face_flux(states[2], states[3], 2)
        top = face_flux(states[4], states[5], 2)
        total = []
        for f in range(NF):
            flux2 = up(flux0[f], top[f])
            fine_ref[f, :, pl.ds(h * LANES, LANES)] = part_ref[f, h] - STEP_RATIO * (flux1[f] - flux0[f])
            fine_ref[f, :, pl.ds((2 + h) * LANES, LANES)] = part_ref[f, 2 + h] - STEP_RATIO * (flux2 - flux1[f])
            total.append(-STEP_RATIO * (flux2 - flux0[f]))
        sums.append(jnp.concatenate(total, axis=0))
    moved = jnp.dot(
        jnp.concatenate(sums, axis=1), mean_ref[: 2 * LANES], precision=HIGHEST, preferred_element_type=jnp.float32
    )
    cell = row * LANES + lane
    for f in range(NF):
        value = coarse_ref[f] + moved[f * 8 : f * 8 + 8]
        turned = value
        for bit in (1, 2, 4):
            turned = jnp.where(row & bit != 0, lane_roll(turned, bit * CYCLE), turned)
        flat = jnp.zeros((8, LANES), jnp.float32)
        for s in range(3):
            shifted = turned if s == 0 else pltpu.roll(turned, 8 - s, 0)
            flat = jnp.where(cell // CYCLE == row + s, shifted, flat)
        for t in range(6):
            out_ref[f, :, pl.ds(t * LANES, LANES)] = flat[t : t + 1]
        out_ref[f, :, pl.ds(6 * LANES, 8 * CYCLE - 6 * LANES)] = flat[6:7, : 8 * CYCLE - 6 * LANES]


def call(kernel, outs, in_spaces, name, flops, scratch=()):
    single = not isinstance(outs, list)
    shapes = [jax.ShapeDtypeStruct(s, jnp.float32) for s in ([outs] if single else outs)]
    specs = [pl.BlockSpec(memory_space=pltpu.VMEM) for _ in shapes]
    return pl.pallas_call(
        kernel,
        out_shape=shapes[0] if single else shapes,
        in_specs=[pl.BlockSpec(memory_space=space) for space in in_spaces],
        out_specs=specs[0] if single else specs,
        scratch_shapes=list(scratch),
        cost_estimate=pl.CostEstimate(flops=flops, bytes_accessed=500_000, transcendentals=0),
        compiler_params=pltpu.CompilerParams(vmem_limit_bytes=16 * 1024 * 1024),
        name=name,
    )


def passed_along(value, axis, steps):
    count = lax.axis_size(axis)
    return lax.ppermute(value, axis, [(source, (source + steps) % count) for source in range(count)])


def local(old_boxes, send_slot, arrival, coarse, coarse_flux):
    V, S = (pltpu.VMEM, pltpu.SMEM)
    ghost_m, mean_m, register_m = (jnp.asarray(m) for m in selection_matrices())
    half_axis = lax.axis_size("gx") // 2
    peers = send_slot.shape[2]
    boxes = jnp.transpose(old_boxes[0, 0], (1, 0, 2))
    outgoing = call(pack_kernel, (peers, 2 * ROWS, LANES), [S, V], "pack", 1_000_000)(
        send_slot[0, 0].T, boxes
    )
    received = lax.all_to_all(outgoing, "gy", split_axis=0, concat_axis=0, tiled=True)
    received = received.reshape(peers * 2 * ROWS, LANES)
    arrive = arrival[0]

    block = passed_along(jnp.transpose(coarse[0], (1, 0, 2)), "gx", half_axis)
    register = passed_along(jnp.transpose(coarse_flux[0], (1, 0, 2)), "gx", half_axis)
    ghosts, base = call(ghost_kernel, [(NF, 3, 8, LANES), (NF, 8, LANES)], [V] * 4, "ghosts", 10_000_000)(
        block, register, ghost_m, register_m
    )
    lowest = lax.dynamic_slice_in_dim(received, arrive[0, 0] * ROWS, ROWS, axis=0)
    highest = lax.dynamic_slice_in_dim(received, arrive[0, 7] * ROWS, ROWS, axis=0)
    before = passed_along(highest, "gy", 1)
    after = passed_along(lowest, "gy", -1)
    part, prim, summed = call(
        side_kernel,
        [(NF, 4, 8, LANES), (NF, 4, 8, LANES), (NF, 8, LANES)],
        [S, V, V, V, V],
        "sides",
        50_000_000,
        [pltpu.VMEM((NF, 4, 8, LANES), jnp.float32)],
    )(arrive, received, ghosts, base, mean_m)
    fine, block_new = call(
        column_kernel, [(NF, 8, 4 * LANES), (NF, 1, 8 * CYCLE)], [V] * 6, "column", 20_000_000
    )(before, after, part, prim, summed, mean_m)
    back = passed_along(block_new, "gx", half_axis)
    return (jnp.transpose(fine, (1, 0, 2))[None, None], jnp.transpose(back, (1, 0, 2))[None])


def solution(mesh):
    return jax.shard_map(
        local,
        mesh=mesh,
        in_specs=(
            P("gx", "gy", None, None, None),
            P("gx", "gy", None, None),
            P("gx", "gy", None),
            P("gx", "gy", None, None),
            P("gx", "gy", None, None),
        ),
        out_specs=(P("gx", "gy", None, None, None), P("gx", "gy", None, None)),
        check_vma=False,
    )
```

```python
import jax
import jax.numpy as jnp
import numpy as np
from jax import lax
from jax.experimental import pallas as pl
from jax.experimental.pallas import tpu as pltpu
from jax.sharding import PartitionSpec as P

NF = 5
BXY = 16
EDGE = BXY // 2 + 2
CYCLE = EDGE * EDGE
LANES = 128
STRIDE = 24
FACES_AT = 896
ROWS = 20
STEP_RATIO = 0.1
HIGHEST = lax.Precision.HIGHEST


def lane_iota():
    return lax.broadcasted_iota(jnp.int32, (8, LANES), 1)


def selection_matrices():
    ghost = np.zeros((LANES, 3 * LANES), np.float32)
    mean = np.zeros((5 * LANES, LANES), np.float32)
    for y in range(BXY):
        for x in range(BXY):
            lane = y * BXY + x
            cy, cx = (1 + y // 2, 1 + x // 2)
            mean[lane, cy * EDGE + cx] = 1.0 / 8.0
            if x == 0:
                ghost[cy * EDGE, lane] = 1.0
                mean[2 * LANES + lane, cy * EDGE] = -0.25
            if x == BXY - 1:
                ghost[cy * EDGE + EDGE - 1, lane] = 1.0
                mean[2 * LANES + lane, cy * EDGE + EDGE - 1] = 0.25
            if y == 0:
                ghost[cx, 2 * LANES + x] = 1.0
                mean[4 * LANES + x, cx] = -0.25
            if y == BXY - 1:
                ghost[(EDGE - 1) * EDGE + cx, 2 * LANES + LANES - BXY + x] = 1.0
                mean[4 * LANES + LANES - BXY + x, (EDGE - 1) * EDGE + cx] = 0.25
    register = np.zeros((LANES, LANES), np.float32)
    for t in range(BXY // 2):
        register[t, (1 + t) * EDGE] = 1.0
        register[8 + t, (1 + t) * EDGE + EDGE - 1] = -1.0
        register[16 + t, 1 + t] = 1.0
        register[24 + t, (EDGE - 1) * EDGE + 1 + t] = -1.0
    return (ghost, mean, register)


def minmod(a, b):
    return jnp.maximum(jnp.minimum(a, b), 0.0) + jnp.minimum(jnp.maximum(a, b), 0.0)


def primitive(u):
    inverse = 1.0 / u[0]
    v = [u[i] * inverse for i in (1, 2, 3)]
    pressure = 0.4 * (u[4] - 0.5 * u[0] * (v[0] * v[0] + v[1] * v[1] + v[2] * v[2]))
    return [u[0]] + v + [pressure]


def state_terms(q, normal):
    density, velocity, pressure = (q[0], q[1:4], q[4])
    kinetic = velocity[0] * velocity[0] + velocity[1] * velocity[1] + velocity[2] * velocity[2]
    energy = 2.5 * pressure + 0.5 * density * kinetic
    momentum = [density * v for v in velocity]
    vn = velocity[normal]
    mass = momentum[normal]
    flux = [mass] + [mass * v for v in velocity] + [(energy + pressure) * vn]
    flux[1 + normal] = flux[1 + normal] + pressure
    scaled = 1.4 * pressure
    speed = jnp.abs(vn) + scaled * lax.rsqrt(scaled * density)
    return ([density] + momentum + [energy], flux, speed)


def face_flux(lower, upper, normal):
    cons_l, flux_l, speed_l = state_terms(lower, normal)
    cons_u, flux_u, speed_u = state_terms(upper, normal)
    half = 0.5 * jnp.maximum(speed_l, speed_u)
    return [
        0.5 * (fl + fu) - half * (cu - cl) for fl, fu, cl, cu in zip(flux_l, flux_u, cons_l, cons_u)
    ]


def lane_roll(value, shift):
    return pltpu.roll(value, shift % LANES, 1)


def pack_kernel(slots_hbm, boxes_hbm, coarse_hbm, flux_hbm, out_ref, sides_ref, slots_ref, boxes_ref, coarse_ref, flux_ref, sems):
    cells, faces = (coarse_hbm.shape[2], flux_hbm.shape[2])
    copies = [
        pltpu.make_async_copy(slots_hbm, slots_ref, sems.at[0]),
        pltpu.make_async_copy(boxes_hbm, boxes_ref, sems.at[1]),
        pltpu.make_async_copy(coarse_hbm, coarse_ref, sems.at[2]),
        pltpu.make_async_copy(flux_hbm, flux_ref, sems.at[3]),
    ]
    for one in copies:
        one.start()
    for one in copies:
        one.wait()
    for f in range(NF):
        sides_ref[f, :, pl.ds(0, cells)] = coarse_ref[f]
        sides_ref[f, :, pl.ds(FACES_AT, faces)] = flux_ref[f]
    held = boxes_ref.shape[1]
    row = lax.broadcasted_iota(jnp.int32, (8, LANES), 0)

    def fill(d, carry):
        first = slots_ref[0, d]

        @pl.when(first < held)
        def _():
            slots = (first, jnp.minimum(slots_ref[1, d], held - 1))
            lines = [[boxes_ref[f, pl.ds(slot, 1), :] for f in range(NF)] for slot in slots]
            for t in range(2 * ROWS // 8):
                tile = None
                for i in range(8):
                    c, r = divmod(8 * t + i, ROWS)
                    f, q = divmod(r, 4)
                    line = jnp.broadcast_to(lines[c][f][:, q * LANES : (q + 1) * LANES], (8, LANES))
                    tile = line if tile is None else jnp.where(row == i, line, tile)
                out_ref[d, 8 * t : 8 * t + 8, :] = tile

        return carry

    lax.fori_loop(0, out_ref.shape[0], fill, 0)


def ghost_kernel(sides_ref, ghost_m_ref, register_m_ref, ghosts_ref, base_ref):
    lane = lane_iota()
    row = lax.broadcasted_iota(jnp.int32, (8, LANES), 0)
    on_block = lane < CYCLE
    cy, cx = (lane // EDGE, lane % EDGE)
    interior = (cy >= 1) & (cy <= EDGE - 2) & (cx >= 1) & (cx <= EDGE - 2)
    blocks = []
    registers = []
    for f in range(NF):
        tiles = [sides_ref[f, :, pl.ds(t * LANES, LANES)] for t in range(6)]
        tiles.append(
            jnp.concatenate(
                [sides_ref[f, :, pl.ds(6 * LANES, 8 * CYCLE - 6 * LANES)], jnp.zeros((1, 7 * LANES - 8 * CYCLE), jnp.float32)],
                axis=1,
            )
        )
        rows = []
        for l in range(8):
            start = l * CYCLE
            t, off = divmod(start, LANES)
            first = jnp.broadcast_to(tiles[t], (8, LANES))
            piece = lane_roll(first, -off)
            if off + CYCLE > LANES:
                second = lane_roll(jnp.broadcast_to(tiles[t + 1], (8, LANES)), -off)
                piece = jnp.where(lane < LANES - off, piece, second)
            rows.append(piece)
        block = rows[0]
        for l in range(1, 8):
            block = jnp.where(row == l, rows[l], block)
        blocks.append(block)
        reg = None
        for l in range(8):
            t, off = divmod(l * 32, LANES)
            piece = lane_roll(jnp.broadcast_to(sides_ref[f, :, pl.ds(FACES_AT + t * LANES, LANES)], (8, LANES)), -off)
            reg = piece if reg is None else jnp.where(row == l, piece, reg)
        registers.append(reg)
    safe = [jnp.where(on_block, b, 1.0) for b in blocks]
    prims = jnp.concatenate(primitive(safe), axis=0)
    spread = jnp.dot(prims, ghost_m_ref[...], precision=HIGHEST, preferred_element_type=jnp.float32)
    placed = jnp.dot(
        jnp.concatenate(registers, axis=0), register_m_ref[...], precision=HIGHEST, preferred_element_type=jnp.float32
    )
    for f in range(NF):
        for t in range(3):
            ghosts_ref[f, t] = spread[f * 8 : f * 8 + 8, t * LANES : (t + 1) * LANES]
        kept = jnp.where(on_block & ~interior, blocks[f], 0.0)
        base_ref[f] = kept + (0.5 * STEP_RATIO) * placed[f * 8 : f * 8 + 8]


def side_kernel(arrive_ref, received_ref, ghosts_ref, base_ref, mean_ref, part_ref, prim_ref, coarse_ref, boxes):
    for k in range(8):
        source, c = (arrive_ref[0, k] // 2, arrive_ref[0, k] % 2)
        box = jnp.where(c == 0, received_ref[source, :ROWS, :], received_ref[source, ROWS:, :])
        boxes[k * STRIDE : k * STRIDE + ROWS, :] = box
    lane = lane_iota()
    x = lane % BXY
    first_x, last_x = (x == 0, x == BXY - 1)
    low_y, high_y = (lane < BXY, lane >= LANES - BXY)
    cells = [[boxes[pl.ds(f * 4 + q, 8, stride=STRIDE), :] for f in range(NF)] for q in range(4)]
    prims = [primitive(c) for c in cells]
    ghost = [[ghosts_ref[f, t] for f in range(NF)] for t in range(3)]
    change = []
    x_sides = [None, None]
    for q in range(4):
        h = q % 2
        g = ghost[h]
        lower, upper, top = ([], [], [])
        for f in range(NF):
            p = prims[q][f]
            below = jnp.where(first_x, g[f], lane_roll(p, 1))
            above = jnp.where(last_x, g[f], lane_roll(p, -1))
            half = 0.5 * minmod(p - below, above - p)
            high = p + half
            lower.append(jnp.where(first_x, g[f], lane_roll(high, 1)))
            upper.append(p - half)
            top.append((high, jnp.where(last_x, g[f], p)))
        low_flux = face_flux(lower, upper, 0)
        top_flux = face_flux([t[0] for t in top], [t[1] for t in top], 0)
        change.append(
            [jnp.where(last_x, t, lane_roll(l, -1)) - l for l, t in zip(low_flux, top_flux)]
        )
        side = [jnp.where(first_x, l, jnp.where(last_x, t, 0.0)) for l, t in zip(low_flux, top_flux)]
        x_sides[h] = side if x_sides[h] is None else [a + b for a, b in zip(x_sides[h], side)]
    y_sides = None
    for j in range(2):
        q0, q1 = (2 * j, 2 * j + 1)
        g = ghost[2]
        states = ([], [], [], [], [], [])
        for f in range(NF):
            p0, p1 = (prims[q0][f], prims[q1][f])
            up0, up1 = (lane_roll(p0, BXY), lane_roll(p1, BXY))
            down0, down1 = (lane_roll(p0, -BXY), lane_roll(p1, -BXY))
            below0, below1 = (jnp.where(low_y, g[f], up0), jnp.where(low_y, up0, up1))
            above0, above1 = (jnp.where(high_y, down1, down0), jnp.where(high_y, g[f], down1))
            half0 = 0.5 * minmod(p0 - below0, above0 - p0)
            half1 = 0.5 * minmod(p1 - below1, above1 - p1)
            high0, high1 = (p0 + half0, p1 + half1)
            roll0, roll1 = (lane_roll(high0, BXY), lane_roll(high1, BXY))
            for one_list, value in zip(
                states,
                (
                    jnp.where(low_y, g[f], roll0),
                    p0 - half0,
                    jnp.where(low_y, roll0, roll1),
                    p1 - half1,
                    high1,
                    jnp.where(high_y, g[f], p1),
                ),
            ):
                one_list.append(value)
        flux0 = face_flux(states[0], states[1], 1)
        flux1 = face_flux(states[2], states[3], 1)
        top = face_flux(states[4], states[5], 1)
        for f in range(NF):
            next0, next1 = (lane_roll(flux0[f], -BXY), lane_roll(flux1[f], -BXY))
            change[q0][f] = change[q0][f] + (jnp.where(high_y, next1, next0) - flux0[f])
            change[q1][f] = change[q1][f] + (jnp.where(high_y, top[f], next1) - flux1[f])
        side = [jnp.where(low_y, a, jnp.where(high_y, b, 0.0)) for a, b in zip(flux0, top)]
        y_sides = side if y_sides is None else [a + b for a, b in zip(y_sides, side)]
    parts = [[c - STEP_RATIO * d for c, d in zip(cells[q], change[q])] for q in range(4)]
    for f in range(NF):
        for q in range(4):
            part_ref[f, q] = parts[q][f]
            prim_ref[f, q] = prims[q][f]
    scale = 0.5 * STEP_RATIO
    stacked = jnp.concatenate(
        [
            jnp.concatenate([parts[0][f] + parts[2][f] for f in range(NF)], axis=0),
            jnp.concatenate([parts[1][f] + parts[3][f] for f in range(NF)], axis=0),
            jnp.concatenate([scale * x_sides[0][f] for f in range(NF)], axis=0),
            jnp.concatenate([scale * x_sides[1][f] for f in range(NF)], axis=0),
            jnp.concatenate([scale * y_sides[f] for f in range(NF)], axis=0),
        ],
        axis=1,
    )
    coarse = jnp.dot(stacked, mean_ref[...], precision=HIGHEST, preferred_element_type=jnp.float32)
    for f in range(NF):
        coarse_ref[f] = base_ref[f] + coarse[f * 8 : f * 8 + 8]


def column_kernel(before_ref, after_ref, part_ref, prim_ref, coarse_ref, mean_ref, fine_ref, out_ref):
    lane = lane_iota()
    row = lax.broadcasted_iota(jnp.int32, (8, LANES), 0)
    first, last = (row == 0, row == 7)

    def down(value, edge):
        return jnp.where(first, edge, pltpu.roll(value, 1, 0))

    def up(value, edge):
        return jnp.where(last, edge, pltpu.roll(value, 7, 0))

    before = [primitive([before_ref[f * 4 + q : f * 4 + q + 1, :] for f in range(NF)]) for q in range(4)]
    after = [primitive([after_ref[f * 4 + q : f * 4 + q + 1, :] for f in range(NF)]) for q in range(4)]
    sums = []
    for h in range(2):
        states = ([], [], [], [], [], [])
        for f in range(NF):
            p0, p1 = (prim_ref[f, h], prim_ref[f, 2 + h])
            b0, b1 = (before[h][f], before[2 + h][f])
            a0, a1 = (after[h][f], after[2 + h][f])
            step = p1 - p0
            half0 = 0.5 * minmod(p0 - down(p1, b1), step)
            half1 = 0.5 * minmod(step, up(p0, a0) - p1)
            half_b = 0.5 * minmod(b1 - b0, p0[0:1] - b1)
            half_a = 0.5 * minmod(a0 - p1[7:8], a1 - a0)
            high1 = p1 + half1
            for one_list, value in zip(
                states,
                (down(high1, b1 + half_b), p0 - half0, p0 + half0, p1 - half1, high1[7:8], a0 - half_a),
            ):
                one_list.append(value)
        flux0 = face_flux(states[0], states[1], 2)
        flux1 = face_flux(states[2], states[3], 2)
        top = face_flux(states[4], states[5], 2)
        total = []
        for f in range(NF):
            flux2 = up(flux0[f], top[f])
            fine_ref[f, :, pl.ds(h * LANES, LANES)] = part_ref[f, h] - STEP_RATIO * (flux1[f] - flux0[f])
            fine_ref[f, :, pl.ds((2 + h) * LANES, LANES)] = part_ref[f, 2 + h] - STEP_RATIO * (flux2 - flux1[f])
            total.append(-STEP_RATIO * (flux2 - flux0[f]))
        sums.append(jnp.concatenate(total, axis=0))
    moved = jnp.dot(
        jnp.concatenate(sums, axis=1), mean_ref[: 2 * LANES], precision=HIGHEST, preferred_element_type=jnp.float32
    )
    cell = row * LANES + lane
    for f in range(NF):
        value = coarse_ref[f] + moved[f * 8 : f * 8 + 8]
        turned = value
        for bit in (1, 2, 4):
            turned = jnp.where(row & bit != 0, lane_roll(turned, bit * CYCLE), turned)
        flat = jnp.zeros((8, LANES), jnp.float32)
        for s in range(3):
            shifted = turned if s == 0 else pltpu.roll(turned, 8 - s, 0)
            flat = jnp.where(cell // CYCLE == row + s, shifted, flat)
        for t in range(6):
            out_ref[f, :, pl.ds(t * LANES, LANES)] = flat[t : t + 1]
        out_ref[f, :, pl.ds(6 * LANES, 8 * CYCLE - 6 * LANES)] = flat[6:7, : 8 * CYCLE - 6 * LANES]


def call(kernel, outs, in_spaces, name, flops, scratch=(), vmem=16):
    single = not isinstance(outs, list)
    shapes = [s if isinstance(s, jax.ShapeDtypeStruct) else pltpu.VMEM(s, jnp.float32) for s in ([outs] if single else outs)]
    specs = [pl.BlockSpec(memory_space=pltpu.VMEM) for _ in shapes]
    return pl.pallas_call(
        kernel,
        out_shape=shapes[0] if single else shapes,
        in_specs=[pl.BlockSpec(memory_space=space) for space in in_spaces],
        out_specs=specs[0] if single else specs,
        scratch_shapes=list(scratch),
        cost_estimate=pl.CostEstimate(flops=flops, bytes_accessed=500_000, transcendentals=0),
        compiler_params=pltpu.CompilerParams(vmem_limit_bytes=vmem * 1024 * 1024),
        name=name,
    )


def passed_along(value, axis, steps):
    count = lax.axis_size(axis)
    return lax.ppermute(value, axis, [(source, (source + steps) % count) for source in range(count)])


def local(old_boxes, send_slot, arrival, coarse, coarse_flux):
    V, S, H = (pltpu.VMEM, pltpu.SMEM, pltpu.HBM)
    ghost_m, mean_m, register_m = (jnp.asarray(m) for m in selection_matrices())
    half_axis = lax.axis_size("gx") // 2
    peers = send_slot.shape[2]
    boxes = jnp.transpose(old_boxes[0, 0], (1, 0, 2))
    slots = send_slot[0, 0].T
    block, register = (jnp.transpose(v[0], (1, 0, 2)) for v in (coarse, coarse_flux))
    outgoing, sides = call(
        pack_kernel,
        [(peers, 2 * ROWS, LANES), (NF, 1, FACES_AT + register.shape[2])],
        [H] * 4,
        "pack",
        1_000_000,
        [
            pltpu.SMEM(slots.shape, jnp.int32),
            pltpu.VMEM(boxes.shape, jnp.float32),
            pltpu.VMEM(block.shape, jnp.float32),
            pltpu.VMEM(register.shape, jnp.float32),
            pltpu.SemaphoreType.DMA((4,)),
        ],
    )(*(pltpu.with_memory_space_constraint(v, H) for v in (slots, boxes, block, register)))
    received = lax.all_to_all(outgoing, "gy", split_axis=0, concat_axis=0, tiled=True)
    received = received.reshape(peers * 2 * ROWS, LANES)
    arrive = arrival[0]

    sides = passed_along(sides, "gx", half_axis)
    ghosts, base = call(ghost_kernel, [(NF, 3, 8, LANES), (NF, 8, LANES)], [V] * 3, "ghosts", 10_000_000)(
        sides, ghost_m, register_m
    )
    lowest = lax.dynamic_slice_in_dim(received, arrive[0, 0] * ROWS, ROWS, axis=0)
    highest = lax.dynamic_slice_in_dim(received, arrive[0, 7] * ROWS, ROWS, axis=0)
    before = passed_along(highest, "gy", 1)
    after = passed_along(lowest, "gy", -1)
    part, prim, summed = call(
        side_kernel,
        [(NF, 4, 8, LANES), (NF, 4, 8, LANES), (NF, 8, LANES)],
        [S, V, V, V, V],
        "sides",
        50_000_000,
        [pltpu.VMEM((8 * STRIDE, LANES), jnp.float32)],
    )(arrive, received.reshape(peers, 2 * ROWS, LANES), ghosts, base, mean_m)
    fine, block_new = call(
        column_kernel, [jax.ShapeDtypeStruct((NF, 8, 4 * LANES), jnp.float32), (NF, 1, 8 * CYCLE)], [V] * 6, "column", 20_000_000
    )(before, after, part, prim, summed, mean_m)
    pairs = [[g, g + half_axis] for g in range(half_axis)]
    both = lax.all_gather(jnp.transpose(block_new, (1, 0, 2))[None], "gx", axis_index_groups=pairs)
    back = lax.dynamic_index_in_dim(both, jnp.where(lax.axis_index("gx") < half_axis, 1, 0), 0, keepdims=False)
    return (jnp.transpose(fine, (1, 0, 2))[None, None], back)


def solution(mesh):
    return jax.shard_map(
        local,
        mesh=mesh,
        in_specs=(
            P("gx", "gy", None, None, None),
            P("gx", "gy", None, None),
            P("gx", "gy", None),
            P("gx", "gy", None, None),
            P("gx", "gy", None, None),
        ),
        out_specs=(P("gx", "gy", None, None, None), P("gx", "gy", None, None)),
        check_vma=False,
    )
```

```python
import functools

import jax
import jax.numpy as jnp
import numpy as np
from jax import lax
from jax.experimental import pallas as pl
from jax.experimental.pallas import tpu as pltpu
from jax.sharding import PartitionSpec as P

NF = 5
BXY = 16
EDGE = BXY // 2 + 2
CYCLE = EDGE * EDGE
LANES = 128
STRIDE = 24
FACES_AT = 896
ROWS = 20
STEP_RATIO = 0.1
HIGHEST = lax.Precision.HIGHEST


def lane_iota():
    return lax.broadcasted_iota(jnp.int32, (8, LANES), 1)


def selection_matrices():
    ghost = np.zeros((LANES, 3 * LANES), np.float32)
    mean = np.zeros((5 * LANES, LANES), np.float32)
    for y in range(BXY):
        for x in range(BXY):
            lane = y * BXY + x
            cy, cx = (1 + y // 2, 1 + x // 2)
            mean[lane, cy * EDGE + cx] = 1.0 / 8.0
            if x == 0:
                ghost[cy * EDGE, lane] = 1.0
                mean[2 * LANES + lane, cy * EDGE] = -0.25
            if x == BXY - 1:
                ghost[cy * EDGE + EDGE - 1, lane] = 1.0
                mean[2 * LANES + lane, cy * EDGE + EDGE - 1] = 0.25
            if y == 0:
                ghost[cx, 2 * LANES + x] = 1.0
                mean[4 * LANES + x, cx] = -0.25
            if y == BXY - 1:
                ghost[(EDGE - 1) * EDGE + cx, 2 * LANES + LANES - BXY + x] = 1.0
                mean[4 * LANES + LANES - BXY + x, (EDGE - 1) * EDGE + cx] = 0.25
    register = np.zeros((LANES, LANES), np.float32)
    for t in range(BXY // 2):
        register[t, (1 + t) * EDGE] = 1.0
        register[8 + t, (1 + t) * EDGE + EDGE - 1] = -1.0
        register[16 + t, 1 + t] = 1.0
        register[24 + t, (EDGE - 1) * EDGE + 1 + t] = -1.0
    return (ghost, mean, register)


def minmod(a, b):
    return jnp.maximum(jnp.minimum(a, b), 0.0) + jnp.minimum(jnp.maximum(a, b), 0.0)


def primitive(u):
    inverse = 1.0 / u[0]
    v = [u[i] * inverse for i in (1, 2, 3)]
    pressure = 0.4 * (u[4] - 0.5 * u[0] * (v[0] * v[0] + v[1] * v[1] + v[2] * v[2]))
    return [u[0]] + v + [pressure]


def state_terms(q, normal):
    density, velocity, pressure = (q[0], q[1:4], q[4])
    kinetic = velocity[0] * velocity[0] + velocity[1] * velocity[1] + velocity[2] * velocity[2]
    energy = 2.5 * pressure + 0.5 * density * kinetic
    momentum = [density * v for v in velocity]
    vn = velocity[normal]
    mass = momentum[normal]
    flux = [mass] + [mass * v for v in velocity] + [(energy + pressure) * vn]
    flux[1 + normal] = flux[1 + normal] + pressure
    scaled = 1.4 * pressure
    speed = jnp.abs(vn) + scaled * lax.rsqrt(scaled * density)
    return ([density] + momentum + [energy], flux, speed)


def face_flux(lower, upper, normal):
    cons_l, flux_l, speed_l = state_terms(lower, normal)
    cons_u, flux_u, speed_u = state_terms(upper, normal)
    half = 0.5 * jnp.maximum(speed_l, speed_u)
    return [
        0.5 * (fl + fu) - half * (cu - cl) for fl, fu, cl, cu in zip(flux_l, flux_u, cons_l, cons_u)
    ]


def lane_roll(value, shift):
    return pltpu.roll(value, shift % LANES, 1)


def pack_kernel(slots_hbm, boxes_hbm, coarse_hbm, flux_hbm, out_ref, sides_ref, slots_ref, boxes_ref, coarse_ref, flux_ref, sems):
    cells, faces = (coarse_hbm.shape[2], flux_hbm.shape[2])
    copies = [
        pltpu.make_async_copy(slots_hbm, slots_ref, sems.at[0]),
        pltpu.make_async_copy(boxes_hbm, boxes_ref, sems.at[1]),
        pltpu.make_async_copy(coarse_hbm, coarse_ref, sems.at[2]),
        pltpu.make_async_copy(flux_hbm, flux_ref, sems.at[3]),
    ]
    for one in copies:
        one.start()
    for one in copies:
        one.wait()
    for f in range(NF):
        sides_ref[f, :, pl.ds(0, cells)] = coarse_ref[f]
        sides_ref[f, :, pl.ds(FACES_AT, faces)] = flux_ref[f]
    held = boxes_ref.shape[1]
    row = lax.broadcasted_iota(jnp.int32, (8, LANES), 0)

    for d in range(out_ref.shape[0]):
        slots = [jnp.minimum(slots_ref[c, d], held - 1) for c in range(2)]
        lines = [[boxes_ref[f, pl.ds(slot, 1), :] for f in range(NF)] for slot in slots]
        for t in range(2 * ROWS // 8):
            tile = None
            for i in range(8):
                c, r = divmod(8 * t + i, ROWS)
                f, q = divmod(r, 4)
                line = jnp.broadcast_to(lines[c][f][:, q * LANES : (q + 1) * LANES], (8, LANES))
                tile = line if tile is None else jnp.where(row == i, line, tile)
            out_ref[d, 8 * t : 8 * t + 8, :] = tile


def ghost_kernel(sides_ref, ghost_m_ref, register_m_ref, ghosts_ref, base_ref):
    lane = lane_iota()
    row = lax.broadcasted_iota(jnp.int32, (8, LANES), 0)
    on_block = lane < CYCLE
    cy, cx = (lane // EDGE, lane % EDGE)
    interior = (cy >= 1) & (cy <= EDGE - 2) & (cx >= 1) & (cx <= EDGE - 2)
    blocks = []
    registers = []
    for f in range(NF):
        tiles = [sides_ref[f, :, pl.ds(t * LANES, LANES)] for t in range(6)]
        tiles.append(
            jnp.concatenate(
                [sides_ref[f, :, pl.ds(6 * LANES, 8 * CYCLE - 6 * LANES)], jnp.zeros((1, 7 * LANES - 8 * CYCLE), jnp.float32)],
                axis=1,
            )
        )
        rows = []
        for l in range(8):
            start = l * CYCLE
            t, off = divmod(start, LANES)
            first = jnp.broadcast_to(tiles[t], (8, LANES))
            piece = lane_roll(first, -off)
            if off + CYCLE > LANES:
                second = lane_roll(jnp.broadcast_to(tiles[t + 1], (8, LANES)), -off)
                piece = jnp.where(lane < LANES - off, piece, second)
            rows.append(piece)
        block = rows[0]
        for l in range(1, 8):
            block = jnp.where(row == l, rows[l], block)
        blocks.append(block)
        reg = None
        for l in range(8):
            t, off = divmod(l * 32, LANES)
            piece = lane_roll(jnp.broadcast_to(sides_ref[f, :, pl.ds(FACES_AT + t * LANES, LANES)], (8, LANES)), -off)
            reg = piece if reg is None else jnp.where(row == l, piece, reg)
        registers.append(reg)
    safe = [jnp.where(on_block, b, 1.0) for b in blocks]
    prims = jnp.concatenate(primitive(safe), axis=0)
    spread = jnp.dot(prims, ghost_m_ref[...], precision=HIGHEST, preferred_element_type=jnp.float32)
    placed = jnp.dot(
        jnp.concatenate(registers, axis=0), register_m_ref[...], precision=HIGHEST, preferred_element_type=jnp.float32
    )
    for f in range(NF):
        for t in range(3):
            ghosts_ref[f, t] = spread[f * 8 : f * 8 + 8, t * LANES : (t + 1) * LANES]
        kept = jnp.where(on_block & ~interior, blocks[f], 0.0)
        base_ref[f] = kept + (0.5 * STEP_RATIO) * placed[f * 8 : f * 8 + 8]


def side_kernel(arrive_ref, received_ref, ghosts_ref, base_ref, mean_ref, fine_ref, edge_ref, out_ref, boxes):
    for k in range(8):
        source, c = (arrive_ref[0, k] // 2, arrive_ref[0, k] % 2)
        box = jnp.where(c == 0, received_ref[source, :ROWS, :], received_ref[source, ROWS:, :])
        boxes[k * STRIDE : k * STRIDE + ROWS, :] = box
    lane = lane_iota()
    x = lane % BXY
    first_x, last_x = (x == 0, x == BXY - 1)
    low_y, high_y = (lane < BXY, lane >= LANES - BXY)
    cells = [[boxes[pl.ds(f * 4 + q, 8, stride=STRIDE), :] for f in range(NF)] for q in range(4)]
    prims = [primitive(c) for c in cells]
    ghost = [[ghosts_ref[f, t] for f in range(NF)] for t in range(3)]
    change = []
    x_sides = [None, None]
    for q in range(4):
        h = q % 2
        g = ghost[h]
        lower, upper, top = ([], [], [])
        for f in range(NF):
            p = prims[q][f]
            below = jnp.where(first_x, g[f], lane_roll(p, 1))
            above = jnp.where(last_x, g[f], lane_roll(p, -1))
            half = 0.5 * minmod(p - below, above - p)
            high = p + half
            lower.append(jnp.where(first_x, g[f], lane_roll(high, 1)))
            upper.append(p - half)
            top.append((high, jnp.where(last_x, g[f], p)))
        low_flux = face_flux(lower, upper, 0)
        top_flux = face_flux([t[0] for t in top], [t[1] for t in top], 0)
        change.append(
            [jnp.where(last_x, t, lane_roll(l, -1)) - l for l, t in zip(low_flux, top_flux)]
        )
        side = [jnp.where(first_x, l, jnp.where(last_x, t, 0.0)) for l, t in zip(low_flux, top_flux)]
        x_sides[h] = side if x_sides[h] is None else [a + b for a, b in zip(x_sides[h], side)]
    y_sides = None
    for j in range(2):
        q0, q1 = (2 * j, 2 * j + 1)
        g = ghost[2]
        states = ([], [], [], [], [], [])
        for f in range(NF):
            p0, p1 = (prims[q0][f], prims[q1][f])
            up0, up1 = (lane_roll(p0, BXY), lane_roll(p1, BXY))
            down0, down1 = (lane_roll(p0, -BXY), lane_roll(p1, -BXY))
            below0, below1 = (jnp.where(low_y, g[f], up0), jnp.where(low_y, up0, up1))
            above0, above1 = (jnp.where(high_y, down1, down0), jnp.where(high_y, g[f], down1))
            half0 = 0.5 * minmod(p0 - below0, above0 - p0)
            half1 = 0.5 * minmod(p1 - below1, above1 - p1)
            high0, high1 = (p0 + half0, p1 + half1)
            roll0, roll1 = (lane_roll(high0, BXY), lane_roll(high1, BXY))
            for one_list, value in zip(
                states,
                (
                    jnp.where(low_y, g[f], roll0),
                    p0 - half0,
                    jnp.where(low_y, roll0, roll1),
                    p1 - half1,
                    high1,
                    jnp.where(high_y, g[f], p1),
                ),
            ):
                one_list.append(value)
        flux0 = face_flux(states[0], states[1], 1)
        flux1 = face_flux(states[2], states[3], 1)
        top = face_flux(states[4], states[5], 1)
        for f in range(NF):
            next0, next1 = (lane_roll(flux0[f], -BXY), lane_roll(flux1[f], -BXY))
            change[q0][f] = change[q0][f] + (jnp.where(high_y, next1, next0) - flux0[f])
            change[q1][f] = change[q1][f] + (jnp.where(high_y, top[f], next1) - flux1[f])
        side = [jnp.where(low_y, a, jnp.where(high_y, b, 0.0)) for a, b in zip(flux0, top)]
        y_sides = side if y_sides is None else [a + b for a, b in zip(y_sides, side)]
    row = lax.broadcasted_iota(jnp.int32, (8, LANES), 0)
    for h in range(2):
        states = ([], [], [], [])
        for f in range(NF):
            p0, p1 = (prims[h][f], prims[2 + h][f])
            step, under = (p1 - p0, pltpu.roll(p1, 1, 0))
            half0 = 0.5 * minmod(p0 - under, step)
            half1 = 0.5 * minmod(step, pltpu.roll(p0, 7, 0) - p1)
            for one_list, value in zip(
                states, (pltpu.roll(p1 + half1, 1, 0), p0 - half0, p0 + half0, p1 - half1)
            ):
                one_list.append(value)
        flux0 = [jnp.where(row == 0, 0.0, v) for v in face_flux(states[0], states[1], 2)]
        flux1 = [jnp.where((row == 0) | (row == 7), 0.0, v) for v in face_flux(states[2], states[3], 2)]
        for f in range(NF):
            change[h][f] = change[h][f] + (flux1[f] - flux0[f])
            change[2 + h][f] = change[2 + h][f] + (pltpu.roll(flux0[f], 7, 0) - flux1[f])
    parts = [[c - STEP_RATIO * d for c, d in zip(cells[q], change[q])] for q in range(4)]
    for f in range(NF):
        for q in range(4):
            fine_ref[f, :, pl.ds(q * LANES, LANES)] = parts[q][f]
        low, high = ([prims[h][f] for h in range(2)], [prims[2 + h][f] for h in range(2)])
        bottom = {2: [v[0:1] for v in low], 3: [v[0:1] for v in high], 4: [v[1:2] for v in low]}
        top = {0: [v[6:7] for v in high], 1: [v[7:8] for v in low], 2: [v[7:8] for v in high]}
        for place in range(4):
            for face in range(4):
                have, cell = (bottom, place + face) if face < 2 else (top, place + face - 2)
                if cell in have:
                    for h in range(2):
                        edge_ref[place, f, 2 * face + h : 2 * face + h + 1, :] = have[cell][h]
                else:
                    edge_ref[place, f, 2 * face : 2 * face + 2, :] = jnp.zeros((2, LANES), jnp.float32)
    scale = 0.5 * STEP_RATIO
    stacked = jnp.concatenate(
        [
            jnp.concatenate([parts[0][f] + parts[2][f] for f in range(NF)], axis=0),
            jnp.concatenate([parts[1][f] + parts[3][f] for f in range(NF)], axis=0),
            jnp.concatenate([scale * x_sides[0][f] for f in range(NF)], axis=0),
            jnp.concatenate([scale * x_sides[1][f] for f in range(NF)], axis=0),
            jnp.concatenate([scale * y_sides[f] for f in range(NF)], axis=0),
        ],
        axis=1,
    )
    coarse = jnp.dot(stacked, mean_ref[...], precision=HIGHEST, preferred_element_type=jnp.float32)
    cell = row * LANES + lane
    for f in range(NF):
        value = base_ref[f] + coarse[f * 8 : f * 8 + 8]
        for bit in (1, 2, 4):
            value = jnp.where(row & bit != 0, lane_roll(value, bit * CYCLE), value)
        flat = jnp.zeros((8, LANES), jnp.float32)
        for n in range(3):
            shifted = value if n == 0 else pltpu.roll(value, 8 - n, 0)
            flat = jnp.where(cell // CYCLE == row + n, shifted, flat)
        for t in range(6):
            out_ref[f, :, pl.ds(t * LANES, LANES)] = flat[t : t + 1]
        out_ref[f, :, pl.ds(6 * LANES, 8 * CYCLE - 6 * LANES)] = flat[6:7, : 8 * CYCLE - 6 * LANES]


def edge_kernel(before_ref, after_ref, edge_ref, mean_ref, fine_in, block_in, fine_ref, block_ref):
    lane = lane_iota()
    row = lax.broadcasted_iota(jnp.int32, (8, LANES), 0)
    rims = primitive(
        [
            jnp.concatenate([before_ref[f * 4 : f * 4 + 4, :], after_ref[f * 4 : f * 4 + 4, :]], axis=0)
            for f in range(NF)
        ]
    )
    lower, upper = ([], [])
    for f in range(NF):
        under = jnp.where(row < 4, rims[f], edge_ref[0, f])
        low = jnp.where(row < 2, pltpu.roll(rims[f], 6, 0), edge_ref[1, f])
        high = jnp.where(row >= 6, pltpu.roll(rims[f], 2, 0), edge_ref[2, f])
        over = jnp.where(row >= 4, rims[f], edge_ref[3, f])
        step = high - low
        lower.append(low + 0.5 * minmod(low - under, step))
        upper.append(high - 0.5 * minmod(step, over - high))
    flux = face_flux(lower, upper, 2)
    stacked = jnp.concatenate(flux, axis=0)
    means = [
        jnp.dot(
            stacked, mean_ref[h * LANES : (h + 1) * LANES], precision=HIGHEST, preferred_element_type=jnp.float32
        )
        for h in range(2)
    ]
    tail = 8 * CYCLE - 6 * LANES
    for f in range(NF):
        above = jnp.where(row < 2, pltpu.roll(flux[f], 6, 0), jnp.where(row < 4, 0.0, flux[f]))
        below = jnp.where(row < 4, flux[f], jnp.where(row < 6, 0.0, pltpu.roll(flux[f], 2, 0)))
        change = STEP_RATIO * (below - above)
        for q in range(4):
            at = pl.ds(q * LANES, LANES)
            edges = jnp.where(row == 0, change[q : q + 1], jnp.where(row == 7, change[4 + q : 5 + q], 0.0))
            fine_ref[f, :, at] = fine_in[f, :, at] + edges
        first, last = ([m[f * 8 + r + h : f * 8 + r + h + 1] for h, m in enumerate(means)] for r in (0, 6))
        block_ref[f, :, pl.ds(LANES, 4 * LANES)] = block_in[f, :, pl.ds(LANES, 4 * LANES)]
        block_ref[f, :, pl.ds(0, LANES)] = block_in[f, :, pl.ds(0, LANES)] + STEP_RATIO * (first[0] + first[1])
        turned = lane_roll(jnp.broadcast_to(STEP_RATIO * (last[0] + last[1]), (8, LANES)), 7 * CYCLE)
        at = pl.ds(5 * LANES, LANES)
        block_ref[f, :, at] = block_in[f, :, at] - jnp.where(lane >= 7 * CYCLE - 5 * LANES, turned, 0.0)[0:1]
        at = pl.ds(6 * LANES, tail)
        block_ref[f, :, at] = block_in[f, :, at] - turned[0:1, :tail]


def store_kernel(half, fine_ref, both_ref, fine_hbm, block_hbm, sems):
    partner = jnp.where(lax.axis_index("gx") < half, 1, 0)
    copies = [
        pltpu.make_async_copy(fine_ref, fine_hbm, sems.at[0]),
        pltpu.make_async_copy(both_ref.at[partner], block_hbm, sems.at[1]),
    ]
    for one in copies:
        one.start()
    for one in copies:
        one.wait()


def call(kernel, outs, in_spaces, name, flops, scratch=()):
    single = not isinstance(outs, list)
    shapes = [s if isinstance(s, jax.ShapeDtypeStruct) else pltpu.VMEM(s, jnp.float32) for s in ([outs] if single else outs)]
    specs = [
        pl.BlockSpec(memory_space=pltpu.HBM if isinstance(s, jax.ShapeDtypeStruct) else pltpu.VMEM) for s in shapes
    ]
    return pl.pallas_call(
        kernel,
        out_shape=shapes[0] if single else shapes,
        in_specs=[pl.BlockSpec(memory_space=space) for space in in_spaces],
        out_specs=specs[0] if single else specs,
        scratch_shapes=list(scratch),
        cost_estimate=pl.CostEstimate(flops=flops, bytes_accessed=flops // 100, transcendentals=0),
        compiler_params=pltpu.CompilerParams(vmem_limit_bytes=16 * 1024 * 1024),
        name=name,
    )


def passed_along(value, axis, steps):
    count = lax.axis_size(axis)
    return lax.ppermute(value, axis, [(source, (source + steps) % count) for source in range(count)])


def local(old_boxes, send_slot, arrival, coarse, coarse_flux):
    V, S, H = (pltpu.VMEM, pltpu.SMEM, pltpu.HBM)
    ghost_m, mean_m, register_m = (jnp.asarray(m) for m in selection_matrices())
    half_axis = lax.axis_size("gx") // 2
    peers = send_slot.shape[2]
    boxes = jnp.transpose(old_boxes[0, 0], (1, 0, 2))
    slots = send_slot[0, 0].T
    block, register = (jnp.transpose(v[0], (1, 0, 2)) for v in (coarse, coarse_flux))
    outgoing, sides = call(
        pack_kernel,
        [(peers, 2 * ROWS, LANES), (NF, 1, FACES_AT + register.shape[2])],
        [H] * 4,
        "pack",
        1_000_000,
        [
            pltpu.SMEM(slots.shape, jnp.int32),
            pltpu.VMEM(boxes.shape, jnp.float32),
            pltpu.VMEM(block.shape, jnp.float32),
            pltpu.VMEM(register.shape, jnp.float32),
            pltpu.SemaphoreType.DMA((4,)),
        ],
    )(*(pltpu.with_memory_space_constraint(v, H) for v in (slots, boxes, block, register)))
    received = lax.all_to_all(outgoing, "gy", split_axis=0, concat_axis=0, tiled=True)
    received = received.reshape(peers * 2 * ROWS, LANES)
    arrive = arrival[0]

    sides = passed_along(sides, "gx", half_axis)
    ghosts, base = call(ghost_kernel, [(NF, 3, 8, LANES), (NF, 8, LANES)], [V] * 3, "ghosts", 0)(
        sides, ghost_m, register_m
    )
    lowest = lax.dynamic_slice_in_dim(received, arrive[0, 0] * ROWS, ROWS, axis=0)
    highest = lax.dynamic_slice_in_dim(received, arrive[0, 7] * ROWS, ROWS, axis=0)
    before = passed_along(highest, "gy", 1)
    after = passed_along(lowest, "gy", -1)
    fine_shape, block_shape = ((NF, 8, 4 * LANES), (NF, 1, 8 * CYCLE))
    fine, edge, block_new = call(
        side_kernel,
        [fine_shape, (4, NF, 8, LANES), block_shape],
        [S, V, V, V, V],
        "sides",
        2_000_000_000,
        [pltpu.VMEM((8 * STRIDE, LANES), jnp.float32)],
    )(arrive, received.reshape(peers, 2 * ROWS, LANES), ghosts, base, mean_m)
    fine, block_new = call(
        edge_kernel, [fine_shape, block_shape], [V] * 6, "edges", 20_000_000
    )(before, after, edge, mean_m, fine, block_new)
    pairs = [[g, g + half_axis] for g in range(half_axis)]
    both = lax.all_gather(block_new, "gx", axis_index_groups=pairs)
    fine, back = call(
        functools.partial(store_kernel, half_axis),
        [jax.ShapeDtypeStruct(v, jnp.float32) for v in (fine_shape, block_shape)],
        [V, V],
        "store",
        1_000_000,
        [pltpu.SemaphoreType.DMA((2,))],
    )(fine, pltpu.with_memory_space_constraint(both, V))
    return (jnp.transpose(fine, (1, 0, 2))[None, None], jnp.transpose(back, (1, 0, 2))[None])


def solution(mesh):
    return jax.shard_map(
        local,
        mesh=mesh,
        in_specs=(
            P("gx", "gy", None, None, None),
            P("gx", "gy", None, None),
            P("gx", "gy", None),
            P("gx", "gy", None, None),
            P("gx", "gy", None, None),
        ),
        out_specs=(P("gx", "gy", None, None, None), P("gx", "gy", None, None)),
        check_vma=False,
    )
```

```python
import functools

import jax
import jax.numpy as jnp
import numpy as np
from jax import lax
from jax.experimental import pallas as pl
from jax.experimental.pallas import tpu as pltpu
from jax.sharding import PartitionSpec as P

NF = 5
BXY = 16
EDGE = BXY // 2 + 2
CYCLE = EDGE * EDGE
LANES = 128
STRIDE = 24
FACES_AT = 896
ROWS = 20
STEP_RATIO = 0.1
HIGHEST = lax.Precision.HIGHEST


def lane_iota():
    return lax.broadcasted_iota(jnp.int32, (8, LANES), 1)


def selection_matrices():
    ghost = np.zeros((LANES, 3 * LANES), np.float32)
    mean = np.zeros((5 * LANES, LANES), np.float32)
    for y in range(BXY):
        for x in range(BXY):
            lane = y * BXY + x
            cy, cx = (1 + y // 2, 1 + x // 2)
            mean[lane, cy * EDGE + cx] = 1.0 / 8.0
            if x == 0:
                ghost[cy * EDGE, lane] = 1.0
                mean[2 * LANES + lane, cy * EDGE] = -0.25
            if x == BXY - 1:
                ghost[cy * EDGE + EDGE - 1, lane] = 1.0
                mean[2 * LANES + lane, cy * EDGE + EDGE - 1] = 0.25
            if y == 0:
                ghost[cx, 2 * LANES + x] = 1.0
                mean[4 * LANES + x, cx] = -0.25
            if y == BXY - 1:
                ghost[(EDGE - 1) * EDGE + cx, 2 * LANES + LANES - BXY + x] = 1.0
                mean[4 * LANES + LANES - BXY + x, (EDGE - 1) * EDGE + cx] = 0.25
    register = np.zeros((LANES, LANES), np.float32)
    for t in range(BXY // 2):
        register[t, (1 + t) * EDGE] = 1.0
        register[8 + t, (1 + t) * EDGE + EDGE - 1] = -1.0
        register[16 + t, 1 + t] = 1.0
        register[24 + t, (EDGE - 1) * EDGE + 1 + t] = -1.0
    return (ghost, mean, register)


def minmod(a, b):
    return jnp.maximum(jnp.minimum(a, b), 0.0) + jnp.minimum(jnp.maximum(a, b), 0.0)


def primitive(u):
    inverse = 1.0 / u[0]
    v = [u[i] * inverse for i in (1, 2, 3)]
    pressure = 0.4 * (u[4] - 0.5 * u[0] * (v[0] * v[0] + v[1] * v[1] + v[2] * v[2]))
    return [u[0]] + v + [pressure]


def state_terms(q, normal):
    density, velocity, pressure = (q[0], q[1:4], q[4])
    kinetic = velocity[0] * velocity[0] + velocity[1] * velocity[1] + velocity[2] * velocity[2]
    energy = 2.5 * pressure + 0.5 * density * kinetic
    momentum = [density * v for v in velocity]
    vn = velocity[normal]
    mass = momentum[normal]
    flux = [mass] + [mass * v for v in velocity] + [(energy + pressure) * vn]
    flux[1 + normal] = flux[1 + normal] + pressure
    scaled = 1.4 * pressure
    speed = jnp.abs(vn) + scaled * lax.rsqrt(scaled * density)
    return ([density] + momentum + [energy], flux, speed)


def face_flux(lower, upper, normal):
    cons_l, flux_l, speed_l = state_terms(lower, normal)
    cons_u, flux_u, speed_u = state_terms(upper, normal)
    half = 0.5 * jnp.maximum(speed_l, speed_u)
    return [
        0.5 * (fl + fu) - half * (cu - cl) for fl, fu, cl, cu in zip(flux_l, flux_u, cons_l, cons_u)
    ]


def lane_roll(value, shift):
    return pltpu.roll(value, shift % LANES, 1)


def pack_kernel(slots_hbm, boxes_hbm, coarse_hbm, flux_hbm, out_ref, sides_ref, slots_ref, boxes_ref, coarse_ref, flux_ref, sems):
    cells, faces = (coarse_hbm.shape[2], flux_hbm.shape[2])
    copies = [
        pltpu.make_async_copy(slots_hbm, slots_ref, sems.at[0]),
        pltpu.make_async_copy(boxes_hbm, boxes_ref, sems.at[1]),
        pltpu.make_async_copy(coarse_hbm, coarse_ref, sems.at[2]),
        pltpu.make_async_copy(flux_hbm, flux_ref, sems.at[3]),
    ]
    for one in copies:
        one.start()
    for one in copies:
        one.wait()
    for f in range(NF):
        sides_ref[f, :, pl.ds(0, cells)] = coarse_ref[f]
        sides_ref[f, :, pl.ds(FACES_AT, faces)] = flux_ref[f]
    held = boxes_ref.shape[1]
    row = lax.broadcasted_iota(jnp.int32, (8, LANES), 0)

    for d in range(out_ref.shape[0]):
        slots = [jnp.minimum(slots_ref[c, d], held - 1) for c in range(2)]
        lines = [[boxes_ref[f, pl.ds(slot, 1), :] for f in range(NF)] for slot in slots]
        for t in range(2 * ROWS // 8):
            tile = None
            for i in range(8):
                c, r = divmod(8 * t + i, ROWS)
                f, q = divmod(r, 4)
                line = jnp.broadcast_to(lines[c][f][:, q * LANES : (q + 1) * LANES], (8, LANES))
                tile = line if tile is None else jnp.where(row == i, line, tile)
            out_ref[d, 8 * t : 8 * t + 8, :] = tile


def ghost_kernel(sides_ref, ghost_m_ref, register_m_ref, ghosts_ref, base_ref):
    lane = lane_iota()
    row = lax.broadcasted_iota(jnp.int32, (8, LANES), 0)
    on_block = lane < CYCLE
    cy, cx = (lane // EDGE, lane % EDGE)
    interior = (cy >= 1) & (cy <= EDGE - 2) & (cx >= 1) & (cx <= EDGE - 2)
    blocks = []
    registers = []
    for f in range(NF):
        tiles = [sides_ref[f, :, pl.ds(t * LANES, LANES)] for t in range(6)]
        tiles.append(
            jnp.concatenate(
                [sides_ref[f, :, pl.ds(6 * LANES, 8 * CYCLE - 6 * LANES)], jnp.zeros((1, 7 * LANES - 8 * CYCLE), jnp.float32)],
                axis=1,
            )
        )
        rows = []
        for l in range(8):
            start = l * CYCLE
            t, off = divmod(start, LANES)
            first = jnp.broadcast_to(tiles[t], (8, LANES))
            piece = lane_roll(first, -off)
            if off + CYCLE > LANES:
                second = lane_roll(jnp.broadcast_to(tiles[t + 1], (8, LANES)), -off)
                piece = jnp.where(lane < LANES - off, piece, second)
            rows.append(piece)
        block = rows[0]
        for l in range(1, 8):
            block = jnp.where(row == l, rows[l], block)
        blocks.append(block)
        reg = None
        for l in range(8):
            t, off = divmod(l * 32, LANES)
            piece = lane_roll(jnp.broadcast_to(sides_ref[f, :, pl.ds(FACES_AT + t * LANES, LANES)], (8, LANES)), -off)
            reg = piece if reg is None else jnp.where(row == l, piece, reg)
        registers.append(reg)
    safe = [jnp.where(on_block, b, 1.0) for b in blocks]
    prims = jnp.concatenate(primitive(safe), axis=0)
    spread = jnp.dot(prims, ghost_m_ref[...], precision=HIGHEST, preferred_element_type=jnp.float32)
    placed = jnp.dot(
        jnp.concatenate(registers, axis=0), register_m_ref[...], precision=HIGHEST, preferred_element_type=jnp.float32
    )
    for f in range(NF):
        for t in range(3):
            ghosts_ref[f, t] = spread[f * 8 : f * 8 + 8, t * LANES : (t + 1) * LANES]
        kept = jnp.where(on_block & ~interior, blocks[f], 0.0)
        base_ref[f] = kept + (0.5 * STEP_RATIO) * placed[f * 8 : f * 8 + 8]


def side_kernel(arrive_ref, received_ref, ghosts_ref, base_ref, mean_ref, fine_ref, edge_ref, out_ref, boxes):
    for k in range(8):
        source, c = (arrive_ref[0, k] // 2, arrive_ref[0, k] % 2)
        box = jnp.where(c == 0, received_ref[source, :ROWS, :], received_ref[source, ROWS:, :])
        boxes[k * STRIDE : k * STRIDE + ROWS, :] = box
    lane = lane_iota()
    x = lane % BXY
    first_x, last_x = (x == 0, x == BXY - 1)
    low_y, high_y = (lane < BXY, lane >= LANES - BXY)
    cells = [[boxes[pl.ds(f * 4 + q, 8, stride=STRIDE), :] for f in range(NF)] for q in range(4)]
    prims = [primitive(c) for c in cells]
    ghost = [[ghosts_ref[f, t] for f in range(NF)] for t in range(3)]
    change = []
    x_sides = [None, None]
    for q in range(4):
        h = q % 2
        g = ghost[h]
        lower, upper, top = ([], [], [])
        for f in range(NF):
            p = prims[q][f]
            below = jnp.where(first_x, g[f], lane_roll(p, 1))
            above = jnp.where(last_x, g[f], lane_roll(p, -1))
            half = 0.5 * minmod(p - below, above - p)
            high = p + half
            lower.append(jnp.where(first_x, g[f], lane_roll(high, 1)))
            upper.append(p - half)
            top.append((high, jnp.where(last_x, g[f], p)))
        low_flux = face_flux(lower, upper, 0)
        top_flux = face_flux([t[0] for t in top], [t[1] for t in top], 0)
        change.append(
            [jnp.where(last_x, t, lane_roll(l, -1)) - l for l, t in zip(low_flux, top_flux)]
        )
        side = [jnp.where(first_x, l, jnp.where(last_x, t, 0.0)) for l, t in zip(low_flux, top_flux)]
        x_sides[h] = side if x_sides[h] is None else [a + b for a, b in zip(x_sides[h], side)]
    y_sides = None
    for j in range(2):
        q0, q1 = (2 * j, 2 * j + 1)
        g = ghost[2]
        states = ([], [], [], [], [], [])
        for f in range(NF):
            p0, p1 = (prims[q0][f], prims[q1][f])
            up0, up1 = (lane_roll(p0, BXY), lane_roll(p1, BXY))
            down0, down1 = (lane_roll(p0, -BXY), lane_roll(p1, -BXY))
            below0, below1 = (jnp.where(low_y, g[f], up0), jnp.where(low_y, up0, up1))
            above0, above1 = (jnp.where(high_y, down1, down0), jnp.where(high_y, g[f], down1))
            half0 = 0.5 * minmod(p0 - below0, above0 - p0)
            half1 = 0.5 * minmod(p1 - below1, above1 - p1)
            high0, high1 = (p0 + half0, p1 + half1)
            roll0, roll1 = (lane_roll(high0, BXY), lane_roll(high1, BXY))
            for one_list, value in zip(
                states,
                (
                    jnp.where(low_y, g[f], roll0),
                    p0 - half0,
                    jnp.where(low_y, roll0, roll1),
                    p1 - half1,
                    high1,
                    jnp.where(high_y, g[f], p1),
                ),
            ):
                one_list.append(value)
        flux0 = face_flux(states[0], states[1], 1)
        flux1 = face_flux(states[2], states[3], 1)
        top = face_flux(states[4], states[5], 1)
        for f in range(NF):
            next0, next1 = (lane_roll(flux0[f], -BXY), lane_roll(flux1[f], -BXY))
            change[q0][f] = change[q0][f] + (jnp.where(high_y, next1, next0) - flux0[f])
            change[q1][f] = change[q1][f] + (jnp.where(high_y, top[f], next1) - flux1[f])
        side = [jnp.where(low_y, a, jnp.where(high_y, b, 0.0)) for a, b in zip(flux0, top)]
        y_sides = side if y_sides is None else [a + b for a, b in zip(y_sides, side)]
    row = lax.broadcasted_iota(jnp.int32, (8, LANES), 0)
    for h in range(2):
        states = ([], [], [], [])
        for f in range(NF):
            p0, p1 = (prims[h][f], prims[2 + h][f])
            step, under = (p1 - p0, pltpu.roll(p1, 1, 0))
            half0 = 0.5 * minmod(p0 - under, step)
            half1 = 0.5 * minmod(step, pltpu.roll(p0, 7, 0) - p1)
            for one_list, value in zip(
                states, (pltpu.roll(p1 + half1, 1, 0), p0 - half0, p0 + half0, p1 - half1)
            ):
                one_list.append(value)
        flux0 = [jnp.where(row == 0, 0.0, v) for v in face_flux(states[0], states[1], 2)]
        flux1 = [jnp.where((row == 0) | (row == 7), 0.0, v) for v in face_flux(states[2], states[3], 2)]
        for f in range(NF):
            change[h][f] = change[h][f] + (flux1[f] - flux0[f])
            change[2 + h][f] = change[2 + h][f] + (pltpu.roll(flux0[f], 7, 0) - flux1[f])
    parts = [[c - STEP_RATIO * d for c, d in zip(cells[q], change[q])] for q in range(4)]
    for f in range(NF):
        for q in range(4):
            fine_ref[f, :, pl.ds(q * LANES, LANES)] = parts[q][f]
        low, high = ([prims[h][f] for h in range(2)], [prims[2 + h][f] for h in range(2)])
        bottom = {2: [v[0:1] for v in low], 3: [v[0:1] for v in high], 4: [v[1:2] for v in low]}
        top = {0: [v[6:7] for v in high], 1: [v[7:8] for v in low], 2: [v[7:8] for v in high]}
        for place in range(4):
            for face in range(4):
                have, cell = (bottom, place + face) if face < 2 else (top, place + face - 2)
                if cell in have:
                    for h in range(2):
                        edge_ref[place, f, 2 * face + h : 2 * face + h + 1, :] = have[cell][h]
                else:
                    edge_ref[place, f, 2 * face : 2 * face + 2, :] = jnp.zeros((2, LANES), jnp.float32)
    scale = 0.5 * STEP_RATIO
    stacked = jnp.concatenate(
        [
            jnp.concatenate([parts[0][f] + parts[2][f] for f in range(NF)], axis=0),
            jnp.concatenate([parts[1][f] + parts[3][f] for f in range(NF)], axis=0),
            jnp.concatenate([scale * x_sides[0][f] for f in range(NF)], axis=0),
            jnp.concatenate([scale * x_sides[1][f] for f in range(NF)], axis=0),
            jnp.concatenate([scale * y_sides[f] for f in range(NF)], axis=0),
        ],
        axis=1,
    )
    coarse = jnp.dot(stacked, mean_ref[...], precision=HIGHEST, preferred_element_type=jnp.float32)
    cell = row * LANES + lane
    for f in range(NF):
        value = base_ref[f] + coarse[f * 8 : f * 8 + 8]
        for bit in (1, 2, 4):
            value = jnp.where(row & bit != 0, lane_roll(value, bit * CYCLE), value)
        flat = jnp.zeros((8, LANES), jnp.float32)
        for n in range(3):
            shifted = value if n == 0 else pltpu.roll(value, 8 - n, 0)
            flat = jnp.where(cell // CYCLE == row + n, shifted, flat)
        for t in range(6):
            out_ref[f, :, pl.ds(t * LANES, LANES)] = flat[t : t + 1]
        out_ref[f, :, pl.ds(6 * LANES, 8 * CYCLE - 6 * LANES)] = flat[6:7, : 8 * CYCLE - 6 * LANES]


def edge_kernel(before_ref, after_ref, edge_ref, mean_ref, fine_in, block_in, fine_ref, block_ref):
    lane = lane_iota()
    row = lax.broadcasted_iota(jnp.int32, (8, LANES), 0)
    rims = primitive(
        [
            jnp.concatenate([before_ref[f * 4 : f * 4 + 4, :], after_ref[f * 4 : f * 4 + 4, :]], axis=0)
            for f in range(NF)
        ]
    )
    lower, upper = ([], [])
    for f in range(NF):
        under = jnp.where(row < 4, rims[f], edge_ref[0, f])
        low = jnp.where(row < 2, pltpu.roll(rims[f], 6, 0), edge_ref[1, f])
        high = jnp.where(row >= 6, pltpu.roll(rims[f], 2, 0), edge_ref[2, f])
        over = jnp.where(row >= 4, rims[f], edge_ref[3, f])
        step = high - low
        lower.append(low + 0.5 * minmod(low - under, step))
        upper.append(high - 0.5 * minmod(step, over - high))
    flux = face_flux(lower, upper, 2)
    stacked = jnp.concatenate(flux, axis=0)
    means = [
        jnp.dot(
            stacked, mean_ref[h * LANES : (h + 1) * LANES], precision=HIGHEST, preferred_element_type=jnp.float32
        )
        for h in range(2)
    ]
    tail = 8 * CYCLE - 6 * LANES
    for f in range(NF):
        above = jnp.where(row < 2, pltpu.roll(flux[f], 6, 0), jnp.where(row < 4, 0.0, flux[f]))
        below = jnp.where(row < 4, flux[f], jnp.where(row < 6, 0.0, pltpu.roll(flux[f], 2, 0)))
        change = STEP_RATIO * (below - above)
        for q in range(4):
            at = pl.ds(q * LANES, LANES)
            edges = jnp.where(row == 0, change[q : q + 1], jnp.where(row == 7, change[4 + q : 5 + q], 0.0))
            fine_ref[f, :, at] = fine_in[f, :, at] + edges
        first, last = ([m[f * 8 + r + h : f * 8 + r + h + 1] for h, m in enumerate(means)] for r in (0, 6))
        block_ref[f, :, pl.ds(LANES, 4 * LANES)] = block_in[f, :, pl.ds(LANES, 4 * LANES)]
        block_ref[f, :, pl.ds(0, LANES)] = block_in[f, :, pl.ds(0, LANES)] + STEP_RATIO * (first[0] + first[1])
        turned = lane_roll(jnp.broadcast_to(STEP_RATIO * (last[0] + last[1]), (8, LANES)), 7 * CYCLE)
        at = pl.ds(5 * LANES, LANES)
        block_ref[f, :, at] = block_in[f, :, at] - jnp.where(lane >= 7 * CYCLE - 5 * LANES, turned, 0.0)[0:1]
        at = pl.ds(6 * LANES, tail)
        block_ref[f, :, at] = block_in[f, :, at] - turned[0:1, :tail]


def store_kernel(half, fine_ref, both_ref, fine_hbm, block_hbm, sems):
    partner = jnp.where(lax.axis_index("gx") < half, 1, 0)
    copies = [
        pltpu.make_async_copy(fine_ref, fine_hbm, sems.at[0]),
        pltpu.make_async_copy(both_ref.at[partner], block_hbm, sems.at[1]),
    ]
    for one in copies:
        one.start()
    for one in copies:
        one.wait()


def call(kernel, outs, in_spaces, name, flops, scratch=()):
    single = not isinstance(outs, list)
    shapes = [s if isinstance(s, jax.ShapeDtypeStruct) else pltpu.VMEM(s, jnp.float32) for s in ([outs] if single else outs)]
    specs = [
        pl.BlockSpec(memory_space=pltpu.HBM if isinstance(s, jax.ShapeDtypeStruct) else pltpu.VMEM) for s in shapes
    ]
    return pl.pallas_call(
        kernel,
        out_shape=shapes[0] if single else shapes,
        in_specs=[pl.BlockSpec(memory_space=space) for space in in_spaces],
        out_specs=specs[0] if single else specs,
        scratch_shapes=list(scratch),
        cost_estimate=pl.CostEstimate(flops=flops, bytes_accessed=500_000, transcendentals=0),
        compiler_params=pltpu.CompilerParams(vmem_limit_bytes=16 * 1024 * 1024),
        name=name,
    )


def passed_along(value, axis, steps):
    count = lax.axis_size(axis)
    return lax.ppermute(value, axis, [(source, (source + steps) % count) for source in range(count)])


def local(old_boxes, send_slot, arrival, coarse, coarse_flux):
    V, S, H = (pltpu.VMEM, pltpu.SMEM, pltpu.HBM)
    ghost_m, mean_m, register_m = (jnp.asarray(m) for m in selection_matrices())
    half_axis = lax.axis_size("gx") // 2
    peers = send_slot.shape[2]
    boxes = jnp.transpose(old_boxes[0, 0], (1, 0, 2))
    slots = send_slot[0, 0].T
    block, register = (jnp.transpose(v[0], (1, 0, 2)) for v in (coarse, coarse_flux))
    outgoing, sides = call(
        pack_kernel,
        [(peers, 2 * ROWS, LANES), (NF, 1, FACES_AT + register.shape[2])],
        [H] * 4,
        "pack",
        1_000_000,
        [
            pltpu.SMEM(slots.shape, jnp.int32),
            pltpu.VMEM(boxes.shape, jnp.float32),
            pltpu.VMEM(block.shape, jnp.float32),
            pltpu.VMEM(register.shape, jnp.float32),
            pltpu.SemaphoreType.DMA((4,)),
        ],
    )(*(pltpu.with_memory_space_constraint(v, H) for v in (slots, boxes, block, register)))
    received = lax.all_to_all(outgoing, "gy", split_axis=0, concat_axis=0, tiled=True)
    received = received.reshape(peers * 2 * ROWS, LANES)
    arrive = arrival[0]

    sides = passed_along(sides, "gx", half_axis)
    ghosts, base = call(ghost_kernel, [(NF, 3, 8, LANES), (NF, 8, LANES)], [V] * 3, "ghosts", 10_000_000)(
        sides, ghost_m, register_m
    )
    lowest = lax.dynamic_slice_in_dim(received, arrive[0, 0] * ROWS, ROWS, axis=0)
    highest = lax.dynamic_slice_in_dim(received, arrive[0, 7] * ROWS, ROWS, axis=0)
    before = passed_along(highest, "gy", 1)
    after = passed_along(lowest, "gy", -1)
    fine_shape, block_shape = ((NF, 8, 4 * LANES), (NF, 1, 8 * CYCLE))
    fine, edge, block_new = call(
        side_kernel,
        [fine_shape, (4, NF, 8, LANES), block_shape],
        [S, V, V, V, V],
        "sides",
        50_000_000,
        [pltpu.VMEM((8 * STRIDE, LANES), jnp.float32)],
    )(arrive, received.reshape(peers, 2 * ROWS, LANES), ghosts, base, mean_m)
    fine, block_new = call(
        edge_kernel, [fine_shape, block_shape], [V] * 6, "edges", 20_000_000
    )(before, after, edge, mean_m, fine, block_new)
    pairs = [[g, g + half_axis] for g in range(half_axis)]
    both = lax.all_gather(block_new, "gx", axis_index_groups=pairs)
    fine, back = call(
        functools.partial(store_kernel, half_axis),
        [jax.ShapeDtypeStruct(v, jnp.float32) for v in (fine_shape, block_shape)],
        [V, V],
        "store",
        1_000_000,
        [pltpu.SemaphoreType.DMA((2,))],
    )(fine, pltpu.with_memory_space_constraint(both, V))
    return (jnp.transpose(fine, (1, 0, 2))[None, None], jnp.transpose(back, (1, 0, 2))[None])


def solution(mesh):
    return jax.shard_map(
        local,
        mesh=mesh,
        in_specs=(
            P("gx", "gy", None, None, None),
            P("gx", "gy", None, None),
            P("gx", "gy", None),
            P("gx", "gy", None, None),
            P("gx", "gy", None, None),
        ),
        out_specs=(P("gx", "gy", None, None, None), P("gx", "gy", None, None)),
        check_vma=False,
    )
```

```python
import functools

import jax
import jax.numpy as jnp
import numpy as np
from jax import lax
from jax.experimental import pallas as pl
from jax.experimental.pallas import tpu as pltpu
from jax.sharding import PartitionSpec as P

NF = 5
BXY = 16
EDGE = BXY // 2 + 2
CYCLE = EDGE * EDGE
LANES = 128
STRIDE = 24
FACES_AT = 896
ROWS = 20
STEP_RATIO = 0.1
HIGHEST = lax.Precision.HIGHEST


def lane_iota():
    return lax.broadcasted_iota(jnp.int32, (8, LANES), 1)


def selection_matrices():
    ghost = np.zeros((LANES, 3 * LANES), np.float32)
    mean = np.zeros((5 * LANES, LANES), np.float32)
    for y in range(BXY):
        for x in range(BXY):
            lane = y * BXY + x
            cy, cx = (1 + y // 2, 1 + x // 2)
            mean[lane, cy * EDGE + cx] = 1.0 / 8.0
            if x == 0:
                ghost[cy * EDGE, lane] = 1.0
                mean[2 * LANES + lane, cy * EDGE] = -0.25
            if x == BXY - 1:
                ghost[cy * EDGE + EDGE - 1, lane] = 1.0
                mean[2 * LANES + lane, cy * EDGE + EDGE - 1] = 0.25
            if y == 0:
                ghost[cx, 2 * LANES + x] = 1.0
                mean[4 * LANES + x, cx] = -0.25
            if y == BXY - 1:
                ghost[(EDGE - 1) * EDGE + cx, 2 * LANES + LANES - BXY + x] = 1.0
                mean[4 * LANES + LANES - BXY + x, (EDGE - 1) * EDGE + cx] = 0.25
    register = np.zeros((LANES, LANES), np.float32)
    for t in range(BXY // 2):
        register[t, (1 + t) * EDGE] = 1.0
        register[8 + t, (1 + t) * EDGE + EDGE - 1] = -1.0
        register[16 + t, 1 + t] = 1.0
        register[24 + t, (EDGE - 1) * EDGE + 1 + t] = -1.0
    return (ghost, mean, register)


def minmod(a, b):
    return jnp.maximum(jnp.minimum(a, b), 0.0) + jnp.minimum(jnp.maximum(a, b), 0.0)


def primitive(u):
    inverse = 1.0 / u[0]
    v = [u[i] * inverse for i in (1, 2, 3)]
    pressure = 0.4 * (u[4] - 0.5 * u[0] * (v[0] * v[0] + v[1] * v[1] + v[2] * v[2]))
    return [u[0]] + v + [pressure]


def state_terms(q, normal):
    density, velocity, pressure = (q[0], q[1:4], q[4])
    kinetic = velocity[0] * velocity[0] + velocity[1] * velocity[1] + velocity[2] * velocity[2]
    energy = 2.5 * pressure + 0.5 * density * kinetic
    momentum = [density * v for v in velocity]
    vn = velocity[normal]
    mass = momentum[normal]
    flux = [mass] + [mass * v for v in velocity] + [(energy + pressure) * vn]
    flux[1 + normal] = flux[1 + normal] + pressure
    scaled = 1.4 * pressure
    speed = jnp.abs(vn) + scaled * lax.rsqrt(scaled * density)
    return ([density] + momentum + [energy], flux, speed)


def face_flux(lower, upper, normal):
    cons_l, flux_l, speed_l = state_terms(lower, normal)
    cons_u, flux_u, speed_u = state_terms(upper, normal)
    half = 0.5 * jnp.maximum(speed_l, speed_u)
    return [
        0.5 * (fl + fu) - half * (cu - cl) for fl, fu, cl, cu in zip(flux_l, flux_u, cons_l, cons_u)
    ]


def lane_roll(value, shift):
    return pltpu.roll(value, shift % LANES, 1)


def pack_kernel(slots_hbm, boxes_hbm, coarse_hbm, flux_hbm, out_ref, sides_ref, slots_ref, boxes_ref, coarse_ref, flux_ref, sems):
    cells, faces = (coarse_hbm.shape[2], flux_hbm.shape[2])
    copies = [
        pltpu.make_async_copy(slots_hbm, slots_ref, sems.at[0]),
        pltpu.make_async_copy(boxes_hbm, boxes_ref, sems.at[1]),
        pltpu.make_async_copy(coarse_hbm, coarse_ref, sems.at[2]),
        pltpu.make_async_copy(flux_hbm, flux_ref, sems.at[3]),
    ]
    for one in copies:
        one.start()
    for one in copies:
        one.wait()
    for f in range(NF):
        sides_ref[f, :, pl.ds(0, cells)] = coarse_ref[f]
        sides_ref[f, :, pl.ds(FACES_AT, faces)] = flux_ref[f]
    held = boxes_ref.shape[1]
    row = lax.broadcasted_iota(jnp.int32, (8, LANES), 0)

    for d in range(out_ref.shape[0]):
        slots = [jnp.minimum(slots_ref[c, d], held - 1) for c in range(2)]
        lines = [[boxes_ref[f, pl.ds(slot, 1), :] for f in range(NF)] for slot in slots]
        for t in range(2 * ROWS // 8):
            tile = None
            for i in range(8):
                c, r = divmod(8 * t + i, ROWS)
                f, q = divmod(r, 4)
                line = jnp.broadcast_to(lines[c][f][:, q * LANES : (q + 1) * LANES], (8, LANES))
                tile = line if tile is None else jnp.where(row == i, line, tile)
            out_ref[d, 8 * t : 8 * t + 8, :] = tile


def ghost_kernel(sides_ref, ghost_m_ref, register_m_ref, ghosts_ref, base_ref):
    lane = lane_iota()
    row = lax.broadcasted_iota(jnp.int32, (8, LANES), 0)
    on_block = lane < CYCLE
    cy, cx = (lane // EDGE, lane % EDGE)
    interior = (cy >= 1) & (cy <= EDGE - 2) & (cx >= 1) & (cx <= EDGE - 2)
    blocks = []
    registers = []
    for f in range(NF):
        tiles = [sides_ref[f, :, pl.ds(t * LANES, LANES)] for t in range(6)]
        tiles.append(
            jnp.concatenate(
                [sides_ref[f, :, pl.ds(6 * LANES, 8 * CYCLE - 6 * LANES)], jnp.zeros((1, 7 * LANES - 8 * CYCLE), jnp.float32)],
                axis=1,
            )
        )
        rows = []
        for l in range(8):
            start = l * CYCLE
            t, off = divmod(start, LANES)
            first = jnp.broadcast_to(tiles[t], (8, LANES))
            piece = lane_roll(first, -off)
            if off + CYCLE > LANES:
                second = lane_roll(jnp.broadcast_to(tiles[t + 1], (8, LANES)), -off)
                piece = jnp.where(lane < LANES - off, piece, second)
            rows.append(piece)
        block = rows[0]
        for l in range(1, 8):
            block = jnp.where(row == l, rows[l], block)
        blocks.append(block)
        reg = None
        for l in range(8):
            t, off = divmod(l * 32, LANES)
            piece = lane_roll(jnp.broadcast_to(sides_ref[f, :, pl.ds(FACES_AT + t * LANES, LANES)], (8, LANES)), -off)
            reg = piece if reg is None else jnp.where(row == l, piece, reg)
        registers.append(reg)
    safe = [jnp.where(on_block, b, 1.0) for b in blocks]
    prims = jnp.concatenate(primitive(safe), axis=0)
    spread = jnp.dot(prims, ghost_m_ref[...], precision=HIGHEST, preferred_element_type=jnp.float32)
    placed = jnp.dot(
        jnp.concatenate(registers, axis=0), register_m_ref[...], precision=HIGHEST, preferred_element_type=jnp.float32
    )
    for f in range(NF):
        for t in range(3):
            ghosts_ref[f, t] = spread[f * 8 : f * 8 + 8, t * LANES : (t + 1) * LANES]
        kept = jnp.where(on_block & ~interior, blocks[f], 0.0)
        base_ref[f] = kept + (0.5 * STEP_RATIO) * placed[f * 8 : f * 8 + 8]


def side_kernel(arrive_ref, received_ref, ghosts_ref, base_ref, mean_ref, fine_ref, edge_ref, out_ref, boxes):
    for k in range(8):
        source, c = (arrive_ref[0, k] // 2, arrive_ref[0, k] % 2)
        box = jnp.where(c == 0, received_ref[source, :ROWS, :], received_ref[source, ROWS:, :])
        boxes[k * STRIDE : k * STRIDE + ROWS, :] = box
    lane = lane_iota()
    x = lane % BXY
    first_x, last_x = (x == 0, x == BXY - 1)
    low_y, high_y = (lane < BXY, lane >= LANES - BXY)
    cells = [[boxes[pl.ds(f * 4 + q, 8, stride=STRIDE), :] for f in range(NF)] for q in range(4)]
    prims = [primitive(c) for c in cells]
    ghost = [[ghosts_ref[f, t] for f in range(NF)] for t in range(3)]
    change = []
    x_sides = [None, None]
    for q in range(4):
        h = q % 2
        g = ghost[h]
        lower, upper, top = ([], [], [])
        for f in range(NF):
            p = prims[q][f]
            below = jnp.where(first_x, g[f], lane_roll(p, 1))
            above = jnp.where(last_x, g[f], lane_roll(p, -1))
            half = 0.5 * minmod(p - below, above - p)
            high = p + half
            lower.append(jnp.where(first_x, g[f], lane_roll(high, 1)))
            upper.append(p - half)
            top.append((high, jnp.where(last_x, g[f], p)))
        low_flux = face_flux(lower, upper, 0)
        top_flux = face_flux([t[0] for t in top], [t[1] for t in top], 0)
        change.append(
            [jnp.where(last_x, t, lane_roll(l, -1)) - l for l, t in zip(low_flux, top_flux)]
        )
        side = [jnp.where(first_x, l, jnp.where(last_x, t, 0.0)) for l, t in zip(low_flux, top_flux)]
        x_sides[h] = side if x_sides[h] is None else [a + b for a, b in zip(x_sides[h], side)]
    y_sides = None
    for j in range(2):
        q0, q1 = (2 * j, 2 * j + 1)
        g = ghost[2]
        states = ([], [], [], [], [], [])
        for f in range(NF):
            p0, p1 = (prims[q0][f], prims[q1][f])
            up0, up1 = (lane_roll(p0, BXY), lane_roll(p1, BXY))
            down0, down1 = (lane_roll(p0, -BXY), lane_roll(p1, -BXY))
            below0, below1 = (jnp.where(low_y, g[f], up0), jnp.where(low_y, up0, up1))
            above0, above1 = (jnp.where(high_y, down1, down0), jnp.where(high_y, g[f], down1))
            half0 = 0.5 * minmod(p0 - below0, above0 - p0)
            half1 = 0.5 * minmod(p1 - below1, above1 - p1)
            high0, high1 = (p0 + half0, p1 + half1)
            roll0, roll1 = (lane_roll(high0, BXY), lane_roll(high1, BXY))
            for one_list, value in zip(
                states,
                (
                    jnp.where(low_y, g[f], roll0),
                    p0 - half0,
                    jnp.where(low_y, roll0, roll1),
                    p1 - half1,
                    high1,
                    jnp.where(high_y, g[f], p1),
                ),
            ):
                one_list.append(value)
        flux0 = face_flux(states[0], states[1], 1)
        flux1 = face_flux(states[2], states[3], 1)
        top = face_flux(states[4], states[5], 1)
        for f in range(NF):
            next0, next1 = (lane_roll(flux0[f], -BXY), lane_roll(flux1[f], -BXY))
            change[q0][f] = change[q0][f] + (jnp.where(high_y, next1, next0) - flux0[f])
            change[q1][f] = change[q1][f] + (jnp.where(high_y, top[f], next1) - flux1[f])
        side = [jnp.where(low_y, a, jnp.where(high_y, b, 0.0)) for a, b in zip(flux0, top)]
        y_sides = side if y_sides is None else [a + b for a, b in zip(y_sides, side)]
    row = lax.broadcasted_iota(jnp.int32, (8, LANES), 0)
    for h in range(2):
        states = ([], [], [], [])
        for f in range(NF):
            p0, p1 = (prims[h][f], prims[2 + h][f])
            step, under = (p1 - p0, pltpu.roll(p1, 1, 0))
            half0 = 0.5 * minmod(p0 - under, step)
            half1 = 0.5 * minmod(step, pltpu.roll(p0, 7, 0) - p1)
            for one_list, value in zip(
                states, (pltpu.roll(p1 + half1, 1, 0), p0 - half0, p0 + half0, p1 - half1)
            ):
                one_list.append(value)
        flux0 = [jnp.where(row == 0, 0.0, v) for v in face_flux(states[0], states[1], 2)]
        flux1 = [jnp.where((row == 0) | (row == 7), 0.0, v) for v in face_flux(states[2], states[3], 2)]
        for f in range(NF):
            change[h][f] = change[h][f] + (flux1[f] - flux0[f])
            change[2 + h][f] = change[2 + h][f] + (pltpu.roll(flux0[f], 7, 0) - flux1[f])
    parts = [[c - STEP_RATIO * d for c, d in zip(cells[q], change[q])] for q in range(4)]
    for f in range(NF):
        for q in range(4):
            fine_ref[f, :, pl.ds(q * LANES, LANES)] = parts[q][f]
        low, high = ([prims[h][f] for h in range(2)], [prims[2 + h][f] for h in range(2)])
        bottom = {2: [v[0:1] for v in low], 3: [v[0:1] for v in high], 4: [v[1:2] for v in low]}
        top = {0: [v[6:7] for v in high], 1: [v[7:8] for v in low], 2: [v[7:8] for v in high]}
        for place in range(4):
            for face in range(4):
                have, cell = (bottom, place + face) if face < 2 else (top, place + face - 2)
                if cell in have:
                    for h in range(2):
                        edge_ref[place, f, 2 * face + h : 2 * face + h + 1, :] = have[cell][h]
                else:
                    edge_ref[place, f, 2 * face : 2 * face + 2, :] = jnp.zeros((2, LANES), jnp.float32)
    scale = 0.5 * STEP_RATIO
    stacked = jnp.concatenate(
        [
            jnp.concatenate([parts[0][f] + parts[2][f] for f in range(NF)], axis=0),
            jnp.concatenate([parts[1][f] + parts[3][f] for f in range(NF)], axis=0),
            jnp.concatenate([scale * x_sides[0][f] for f in range(NF)], axis=0),
            jnp.concatenate([scale * x_sides[1][f] for f in range(NF)], axis=0),
            jnp.concatenate([scale * y_sides[f] for f in range(NF)], axis=0),
        ],
        axis=1,
    )
    coarse = jnp.dot(stacked, mean_ref[...], precision=HIGHEST, preferred_element_type=jnp.float32)
    cell = row * LANES + lane
    for f in range(NF):
        value = base_ref[f] + coarse[f * 8 : f * 8 + 8]
        for bit in (1, 2, 4):
            value = jnp.where(row & bit != 0, lane_roll(value, bit * CYCLE), value)
        flat = jnp.zeros((8, LANES), jnp.float32)
        for n in range(3):
            shifted = value if n == 0 else pltpu.roll(value, 8 - n, 0)
            flat = jnp.where(cell // CYCLE == row + n, shifted, flat)
        for t in range(6):
            out_ref[f, :, pl.ds(t * LANES, LANES)] = flat[t : t + 1]
        out_ref[f, :, pl.ds(6 * LANES, 8 * CYCLE - 6 * LANES)] = flat[6:7, : 8 * CYCLE - 6 * LANES]


def edge_kernel(before_ref, after_ref, edge_ref, mean_ref, fine_in, block_in, fine_ref, block_ref):
    lane = lane_iota()
    row = lax.broadcasted_iota(jnp.int32, (8, LANES), 0)
    rims = primitive(
        [
            jnp.concatenate([before_ref[f * 4 : f * 4 + 4, :], after_ref[f * 4 : f * 4 + 4, :]], axis=0)
            for f in range(NF)
        ]
    )
    lower, upper = ([], [])
    for f in range(NF):
        under = jnp.where(row < 4, rims[f], edge_ref[0, f])
        low = jnp.where(row < 2, pltpu.roll(rims[f], 6, 0), edge_ref[1, f])
        high = jnp.where(row >= 6, pltpu.roll(rims[f], 2, 0), edge_ref[2, f])
        over = jnp.where(row >= 4, rims[f], edge_ref[3, f])
        step = high - low
        lower.append(low + 0.5 * minmod(low - under, step))
        upper.append(high - 0.5 * minmod(step, over - high))
    flux = face_flux(lower, upper, 2)
    stacked = jnp.concatenate(flux, axis=0)
    means = [
        jnp.dot(
            stacked, mean_ref[h * LANES : (h + 1) * LANES], precision=HIGHEST, preferred_element_type=jnp.float32
        )
        for h in range(2)
    ]
    tail = 8 * CYCLE - 6 * LANES
    for f in range(NF):
        above = jnp.where(row < 2, pltpu.roll(flux[f], 6, 0), jnp.where(row < 4, 0.0, flux[f]))
        below = jnp.where(row < 4, flux[f], jnp.where(row < 6, 0.0, pltpu.roll(flux[f], 2, 0)))
        change = STEP_RATIO * (below - above)
        for q in range(4):
            at = pl.ds(q * LANES, LANES)
            edges = jnp.where(row == 0, change[q : q + 1], jnp.where(row == 7, change[4 + q : 5 + q], 0.0))
            fine_ref[f, :, at] = fine_in[f, :, at] + edges
        first, last = ([m[f * 8 + r + h : f * 8 + r + h + 1] for h, m in enumerate(means)] for r in (0, 6))
        block_ref[f, :, pl.ds(LANES, 4 * LANES)] = block_in[f, :, pl.ds(LANES, 4 * LANES)]
        block_ref[f, :, pl.ds(0, LANES)] = block_in[f, :, pl.ds(0, LANES)] + STEP_RATIO * (first[0] + first[1])
        turned = lane_roll(jnp.broadcast_to(STEP_RATIO * (last[0] + last[1]), (8, LANES)), 7 * CYCLE)
        at = pl.ds(5 * LANES, LANES)
        block_ref[f, :, at] = block_in[f, :, at] - jnp.where(lane >= 7 * CYCLE - 5 * LANES, turned, 0.0)[0:1]
        at = pl.ds(6 * LANES, tail)
        block_ref[f, :, at] = block_in[f, :, at] - turned[0:1, :tail]


def store_kernel(half, fine_ref, both_ref, fine_hbm, block_hbm, sems):
    partner = jnp.where(lax.axis_index("gx") < half, 1, 0)
    copies = [
        pltpu.make_async_copy(fine_ref, fine_hbm, sems.at[0]),
        pltpu.make_async_copy(both_ref.at[partner], block_hbm, sems.at[1]),
    ]
    for one in copies:
        one.start()
    for one in copies:
        one.wait()


def call(kernel, outs, in_spaces, name, flops, scratch=()):
    single = not isinstance(outs, list)
    shapes = [s if isinstance(s, jax.ShapeDtypeStruct) else pltpu.VMEM(s, jnp.float32) for s in ([outs] if single else outs)]
    specs = [
        pl.BlockSpec(memory_space=pltpu.HBM if isinstance(s, jax.ShapeDtypeStruct) else pltpu.VMEM) for s in shapes
    ]
    return pl.pallas_call(
        kernel,
        out_shape=shapes[0] if single else shapes,
        in_specs=[pl.BlockSpec(memory_space=space) for space in in_spaces],
        out_specs=specs[0] if single else specs,
        scratch_shapes=list(scratch),
        cost_estimate=pl.CostEstimate(flops=flops, bytes_accessed=500_000, transcendentals=0),
        compiler_params=pltpu.CompilerParams(vmem_limit_bytes=16 * 1024 * 1024),
        name=name,
    )


def passed_along(value, axis, steps):
    count = lax.axis_size(axis)
    return lax.ppermute(value, axis, [(source, (source + steps) % count) for source in range(count)])


def local(old_boxes, send_slot, arrival, coarse, coarse_flux):
    V, S, H = (pltpu.VMEM, pltpu.SMEM, pltpu.HBM)
    ghost_m, mean_m, register_m = (jnp.asarray(m) for m in selection_matrices())
    half_axis = lax.axis_size("gx") // 2
    peers = send_slot.shape[2]
    boxes = jnp.transpose(old_boxes[0, 0], (1, 0, 2))
    slots = send_slot[0, 0].T
    block, register = (jnp.transpose(v[0], (1, 0, 2)) for v in (coarse, coarse_flux))
    outgoing, sides = call(
        pack_kernel,
        [(peers, 2 * ROWS, LANES), (NF, 1, FACES_AT + register.shape[2])],
        [H] * 4,
        "pack",
        1_000_000,
        [
            pltpu.SMEM(slots.shape, jnp.int32),
            pltpu.VMEM(boxes.shape, jnp.float32),
            pltpu.VMEM(block.shape, jnp.float32),
            pltpu.VMEM(register.shape, jnp.float32),
            pltpu.SemaphoreType.DMA((4,)),
        ],
    )(*(pltpu.with_memory_space_constraint(v, H) for v in (slots, boxes, block, register)))
    received = lax.all_to_all(outgoing, "gy", split_axis=0, concat_axis=0, tiled=True)
    received = received.reshape(peers * 2 * ROWS, LANES)
    arrive = arrival[0]

    sides = passed_along(sides, "gx", half_axis)
    ghosts, base = call(ghost_kernel, [(NF, 3, 8, LANES), (NF, 8, LANES)], [V] * 3, "ghosts", 10_000_000)(
        sides, ghost_m, register_m
    )
    lowest = lax.dynamic_slice_in_dim(received, arrive[0, 0] * ROWS, ROWS, axis=0)
    highest = lax.dynamic_slice_in_dim(received, arrive[0, 7] * ROWS, ROWS, axis=0)
    before = passed_along(highest, "gy", 1)
    after = passed_along(lowest, "gy", -1)
    fine_shape, block_shape = ((NF, 8, 4 * LANES), (NF, 1, 8 * CYCLE))
    fine, edge, block_new = call(
        side_kernel,
        [fine_shape, (4, NF, 8, LANES), block_shape],
        [S, V, V, V, V],
        "sides",
        50_000_000,
        [pltpu.VMEM((9 * STRIDE, LANES), jnp.float32)],
    )(arrive, received.reshape(peers, 2 * ROWS, LANES), ghosts, base, mean_m)
    fine, block_new = call(
        edge_kernel, [fine_shape, block_shape], [V] * 6, "edges", 20_000_000
    )(before, after, edge, mean_m, fine, block_new)
    pairs = [[g, g + half_axis] for g in range(half_axis)]
    both = lax.all_gather(block_new, "gx", axis_index_groups=pairs)
    fine, back = call(
        functools.partial(store_kernel, half_axis),
        [jax.ShapeDtypeStruct(v, jnp.float32) for v in (fine_shape, block_shape)],
        [V, V],
        "store",
        1_000_000,
        [pltpu.SemaphoreType.DMA((2,))],
    )(fine, pltpu.with_memory_space_constraint(both, V))
    return (jnp.transpose(fine, (1, 0, 2))[None, None], jnp.transpose(back, (1, 0, 2))[None])


def solution(mesh):
    return jax.shard_map(
        local,
        mesh=mesh,
        in_specs=(
            P("gx", "gy", None, None, None),
            P("gx", "gy", None, None),
            P("gx", "gy", None),
            P("gx", "gy", None, None),
            P("gx", "gy", None, None),
        ),
        out_specs=(P("gx", "gy", None, None, None), P("gx", "gy", None, None)),
        check_vma=False,
    )
```

```python
import functools

import jax
import jax.numpy as jnp
import numpy as np
from jax import lax
from jax.experimental import pallas as pl
from jax.experimental.pallas import tpu as pltpu
from jax.sharding import PartitionSpec as P

NF = 5
BXY = 16
EDGE = BXY // 2 + 2
CYCLE = EDGE * EDGE
LANES = 128
STRIDE = 24
FACES_AT = 896
ROWS = 20
STEP_RATIO = 0.1
HIGHEST = lax.Precision.HIGHEST


def lane_iota():
    return lax.broadcasted_iota(jnp.int32, (8, LANES), 1)


def selection_matrices():
    ghost = np.zeros((LANES, 3 * LANES), np.float32)
    mean = np.zeros((5 * LANES, LANES), np.float32)
    for y in range(BXY):
        for x in range(BXY):
            lane = y * BXY + x
            cy, cx = (1 + y // 2, 1 + x // 2)
            mean[lane, cy * EDGE + cx] = 1.0 / 8.0
            if x == 0:
                ghost[cy * EDGE, lane] = 1.0
                mean[2 * LANES + lane, cy * EDGE] = -0.25
            if x == BXY - 1:
                ghost[cy * EDGE + EDGE - 1, lane] = 1.0
                mean[2 * LANES + lane, cy * EDGE + EDGE - 1] = 0.25
            if y == 0:
                ghost[cx, 2 * LANES + x] = 1.0
                mean[4 * LANES + x, cx] = -0.25
            if y == BXY - 1:
                ghost[(EDGE - 1) * EDGE + cx, 2 * LANES + LANES - BXY + x] = 1.0
                mean[4 * LANES + LANES - BXY + x, (EDGE - 1) * EDGE + cx] = 0.25
    register = np.zeros((LANES, LANES), np.float32)
    for t in range(BXY // 2):
        register[t, (1 + t) * EDGE] = 1.0
        register[8 + t, (1 + t) * EDGE + EDGE - 1] = -1.0
        register[16 + t, 1 + t] = 1.0
        register[24 + t, (EDGE - 1) * EDGE + 1 + t] = -1.0
    return (ghost, mean, register)


def minmod(a, b):
    return jnp.maximum(jnp.minimum(a, b), 0.0) + jnp.minimum(jnp.maximum(a, b), 0.0)


def primitive(u):
    inverse = 1.0 / u[0]
    v = [u[i] * inverse for i in (1, 2, 3)]
    pressure = 0.4 * (u[4] - 0.5 * u[0] * (v[0] * v[0] + v[1] * v[1] + v[2] * v[2]))
    return [u[0]] + v + [pressure]


def state_terms(q, normal):
    density, velocity, pressure = (q[0], q[1:4], q[4])
    kinetic = velocity[0] * velocity[0] + velocity[1] * velocity[1] + velocity[2] * velocity[2]
    energy = 2.5 * pressure + 0.5 * density * kinetic
    momentum = [density * v for v in velocity]
    vn = velocity[normal]
    mass = momentum[normal]
    flux = [mass] + [mass * v for v in velocity] + [(energy + pressure) * vn]
    flux[1 + normal] = flux[1 + normal] + pressure
    scaled = 1.4 * pressure
    speed = jnp.abs(vn) + scaled * lax.rsqrt(scaled * density)
    return ([density] + momentum + [energy], flux, speed)


def face_flux(lower, upper, normal):
    cons_l, flux_l, speed_l = state_terms(lower, normal)
    cons_u, flux_u, speed_u = state_terms(upper, normal)
    half = 0.5 * jnp.maximum(speed_l, speed_u)
    return [
        0.5 * (fl + fu) - half * (cu - cl) for fl, fu, cl, cu in zip(flux_l, flux_u, cons_l, cons_u)
    ]


def lane_roll(value, shift):
    return pltpu.roll(value, shift % LANES, 1)


def pack_kernel(slots_hbm, boxes_hbm, coarse_hbm, flux_hbm, out_ref, sides_ref, slots_ref, boxes_ref, coarse_ref, flux_ref, sems):
    cells, faces = (coarse_hbm.shape[2], flux_hbm.shape[2])
    copies = [
        pltpu.make_async_copy(slots_hbm, slots_ref, sems.at[0]),
        pltpu.make_async_copy(boxes_hbm, boxes_ref, sems.at[1]),
        pltpu.make_async_copy(coarse_hbm, coarse_ref, sems.at[2]),
        pltpu.make_async_copy(flux_hbm, flux_ref, sems.at[3]),
    ]
    for one in copies:
        one.start()
    for one in copies:
        one.wait()
    for f in range(NF):
        sides_ref[f, :, pl.ds(0, cells)] = coarse_ref[f]
        sides_ref[f, :, pl.ds(FACES_AT, faces)] = flux_ref[f]
    held = boxes_ref.shape[1]
    row = lax.broadcasted_iota(jnp.int32, (8, LANES), 0)

    for d in range(out_ref.shape[0]):
        slots = [jnp.minimum(slots_ref[c, d], held - 1) for c in range(2)]
        lines = [[boxes_ref[f, pl.ds(slot, 1), :] for f in range(NF)] for slot in slots]
        for t in range(2 * ROWS // 8):
            tile = None
            for i in range(8):
                c, r = divmod(8 * t + i, ROWS)
                f, q = divmod(r, 4)
                line = jnp.broadcast_to(lines[c][f][:, q * LANES : (q + 1) * LANES], (8, LANES))
                tile = line if tile is None else jnp.where(row == i, line, tile)
            out_ref[d, 8 * t : 8 * t + 8, :] = tile


def ghost_kernel(sides_ref, ghost_m_ref, register_m_ref, ghosts_ref, base_ref):
    lane = lane_iota()
    row = lax.broadcasted_iota(jnp.int32, (8, LANES), 0)
    on_block = lane < CYCLE
    cy, cx = (lane // EDGE, lane % EDGE)
    interior = (cy >= 1) & (cy <= EDGE - 2) & (cx >= 1) & (cx <= EDGE - 2)
    blocks = []
    registers = []
    for f in range(NF):
        tiles = [sides_ref[f, :, pl.ds(t * LANES, LANES)] for t in range(6)]
        tiles.append(
            jnp.concatenate(
                [sides_ref[f, :, pl.ds(6 * LANES, 8 * CYCLE - 6 * LANES)], jnp.zeros((1, 7 * LANES - 8 * CYCLE), jnp.float32)],
                axis=1,
            )
        )
        rows = []
        for l in range(8):
            start = l * CYCLE
            t, off = divmod(start, LANES)
            first = jnp.broadcast_to(tiles[t], (8, LANES))
            piece = lane_roll(first, -off)
            if off + CYCLE > LANES:
                second = lane_roll(jnp.broadcast_to(tiles[t + 1], (8, LANES)), -off)
                piece = jnp.where(lane < LANES - off, piece, second)
            rows.append(piece)
        block = rows[0]
        for l in range(1, 8):
            block = jnp.where(row == l, rows[l], block)
        blocks.append(block)
        reg = None
        for l in range(8):
            t, off = divmod(l * 32, LANES)
            piece = lane_roll(jnp.broadcast_to(sides_ref[f, :, pl.ds(FACES_AT + t * LANES, LANES)], (8, LANES)), -off)
            reg = piece if reg is None else jnp.where(row == l, piece, reg)
        registers.append(reg)
    safe = [jnp.where(on_block, b, 1.0) for b in blocks]
    prims = jnp.concatenate(primitive(safe), axis=0)
    spread = jnp.dot(prims, ghost_m_ref[...], precision=HIGHEST, preferred_element_type=jnp.float32)
    placed = jnp.dot(
        jnp.concatenate(registers, axis=0), register_m_ref[...], precision=HIGHEST, preferred_element_type=jnp.float32
    )
    for f in range(NF):
        for t in range(3):
            ghosts_ref[f, t] = spread[f * 8 : f * 8 + 8, t * LANES : (t + 1) * LANES]
        kept = jnp.where(on_block & ~interior, blocks[f], 0.0)
        base_ref[f] = kept + (0.5 * STEP_RATIO) * placed[f * 8 : f * 8 + 8]


def side_kernel(arrive_ref, received_ref, ghosts_ref, base_ref, mean_ref, fine_ref, edge_ref, out_ref, boxes):
    for k in range(8):
        source, c = (arrive_ref[0, k] // 2, arrive_ref[0, k] % 2)
        box = jnp.where(c == 0, received_ref[source, :ROWS, :], received_ref[source, ROWS:, :])
        boxes[k * STRIDE : k * STRIDE + ROWS, :] = box
    lane = lane_iota()
    x = lane % BXY
    first_x, last_x = (x == 0, x == BXY - 1)
    low_y, high_y = (lane < BXY, lane >= LANES - BXY)
    cells = [[boxes[pl.ds(f * 4 + q, 8, stride=STRIDE), :] for f in range(NF)] for q in range(4)]
    prims = [primitive(c) for c in cells]
    ghost = [[ghosts_ref[f, t] for f in range(NF)] for t in range(3)]
    change = []
    x_sides = [None, None]
    for q in range(4):
        h = q % 2
        g = ghost[h]
        lower, upper, top = ([], [], [])
        for f in range(NF):
            p = prims[q][f]
            below = jnp.where(first_x, g[f], lane_roll(p, 1))
            above = jnp.where(last_x, g[f], lane_roll(p, -1))
            half = 0.5 * minmod(p - below, above - p)
            high = p + half
            lower.append(jnp.where(first_x, g[f], lane_roll(high, 1)))
            upper.append(p - half)
            top.append((high, jnp.where(last_x, g[f], p)))
        low_flux = face_flux(lower, upper, 0)
        top_flux = face_flux([t[0] for t in top], [t[1] for t in top], 0)
        change.append(
            [jnp.where(last_x, t, lane_roll(l, -1)) - l for l, t in zip(low_flux, top_flux)]
        )
        side = [jnp.where(first_x, l, jnp.where(last_x, t, 0.0)) for l, t in zip(low_flux, top_flux)]
        x_sides[h] = side if x_sides[h] is None else [a + b for a, b in zip(x_sides[h], side)]
    y_sides = None
    for j in range(2):
        q0, q1 = (2 * j, 2 * j + 1)
        g = ghost[2]
        states = ([], [], [], [], [], [])
        for f in range(NF):
            p0, p1 = (prims[q0][f], prims[q1][f])
            up0, up1 = (lane_roll(p0, BXY), lane_roll(p1, BXY))
            down0, down1 = (lane_roll(p0, -BXY), lane_roll(p1, -BXY))
            below0, below1 = (jnp.where(low_y, g[f], up0), jnp.where(low_y, up0, up1))
            above0, above1 = (jnp.where(high_y, down1, down0), jnp.where(high_y, g[f], down1))
            half0 = 0.5 * minmod(p0 - below0, above0 - p0)
            half1 = 0.5 * minmod(p1 - below1, above1 - p1)
            high0, high1 = (p0 + half0, p1 + half1)
            roll0, roll1 = (lane_roll(high0, BXY), lane_roll(high1, BXY))
            for one_list, value in zip(
                states,
                (
                    jnp.where(low_y, g[f], roll0),
                    p0 - half0,
                    jnp.where(low_y, roll0, roll1),
                    p1 - half1,
                    high1,
                    jnp.where(high_y, g[f], p1),
                ),
            ):
                one_list.append(value)
        flux0 = face_flux(states[0], states[1], 1)
        flux1 = face_flux(states[2], states[3], 1)
        top = face_flux(states[4], states[5], 1)
        for f in range(NF):
            next0, next1 = (lane_roll(flux0[f], -BXY), lane_roll(flux1[f], -BXY))
            change[q0][f] = change[q0][f] + (jnp.where(high_y, next1, next0) - flux0[f])
            change[q1][f] = change[q1][f] + (jnp.where(high_y, top[f], next1) - flux1[f])
        side = [jnp.where(low_y, a, jnp.where(high_y, b, 0.0)) for a, b in zip(flux0, top)]
        y_sides = side if y_sides is None else [a + b for a, b in zip(y_sides, side)]
    row = lax.broadcasted_iota(jnp.int32, (8, LANES), 0)
    for h in range(2):
        states = ([], [], [], [])
        for f in range(NF):
            p0, p1 = (prims[h][f], prims[2 + h][f])
            step, under = (p1 - p0, pltpu.roll(p1, 1, 0))
            half0 = 0.5 * minmod(p0 - under, step)
            half1 = 0.5 * minmod(step, pltpu.roll(p0, 7, 0) - p1)
            for one_list, value in zip(
                states, (pltpu.roll(p1 + half1, 1, 0), p0 - half0, p0 + half0, p1 - half1)
            ):
                one_list.append(value)
        flux0 = [jnp.where(row == 0, 0.0, v) for v in face_flux(states[0], states[1], 2)]
        flux1 = [jnp.where((row == 0) | (row == 7), 0.0, v) for v in face_flux(states[2], states[3], 2)]
        for f in range(NF):
            change[h][f] = change[h][f] + (flux1[f] - flux0[f])
            change[2 + h][f] = change[2 + h][f] + (pltpu.roll(flux0[f], 7, 0) - flux1[f])
    parts = [[c - STEP_RATIO * d for c, d in zip(cells[q], change[q])] for q in range(4)]
    for f in range(NF):
        for q in range(4):
            fine_ref[f, :, pl.ds(q * LANES, LANES)] = parts[q][f]
        low, high = ([prims[h][f] for h in range(2)], [prims[2 + h][f] for h in range(2)])
        bottom = {2: [v[0:1] for v in low], 3: [v[0:1] for v in high], 4: [v[1:2] for v in low]}
        top = {0: [v[6:7] for v in high], 1: [v[7:8] for v in low], 2: [v[7:8] for v in high]}
        for place in range(4):
            for face in range(4):
                have, cell = (bottom, place + face) if face < 2 else (top, place + face - 2)
                if cell in have:
                    for h in range(2):
                        edge_ref[place, f, 2 * face + h : 2 * face + h + 1, :] = have[cell][h]
                else:
                    edge_ref[place, f, 2 * face : 2 * face + 2, :] = jnp.zeros((2, LANES), jnp.float32)
    scale = 0.5 * STEP_RATIO
    stacked = jnp.concatenate(
        [
            jnp.concatenate([parts[0][f] + parts[2][f] for f in range(NF)], axis=0),
            jnp.concatenate([parts[1][f] + parts[3][f] for f in range(NF)], axis=0),
            jnp.concatenate([scale * x_sides[0][f] for f in range(NF)], axis=0),
            jnp.concatenate([scale * x_sides[1][f] for f in range(NF)], axis=0),
            jnp.concatenate([scale * y_sides[f] for f in range(NF)], axis=0),
        ],
        axis=1,
    )
    coarse = jnp.dot(stacked, mean_ref[...], precision=HIGHEST, preferred_element_type=jnp.float32)
    cell = row * LANES + lane
    for f in range(NF):
        value = base_ref[f] + coarse[f * 8 : f * 8 + 8]
        for bit in (1, 2, 4):
            value = jnp.where(row & bit != 0, lane_roll(value, bit * CYCLE), value)
        flat = jnp.zeros((8, LANES), jnp.float32)
        for n in range(3):
            shifted = value if n == 0 else pltpu.roll(value, 8 - n, 0)
            flat = jnp.where(cell // CYCLE == row + n, shifted, flat)
        for t in range(6):
            out_ref[f, :, pl.ds(t * LANES, LANES)] = flat[t : t + 1]
        out_ref[f, :, pl.ds(6 * LANES, 8 * CYCLE - 6 * LANES)] = flat[6:7, : 8 * CYCLE - 6 * LANES]


def edge_kernel(before_ref, after_ref, edge_ref, mean_ref, fine_in, block_in, fine_ref, block_ref):
    lane = lane_iota()
    row = lax.broadcasted_iota(jnp.int32, (8, LANES), 0)
    rims = primitive(
        [
            jnp.concatenate([before_ref[f * 4 : f * 4 + 4, :], after_ref[f * 4 : f * 4 + 4, :]], axis=0)
            for f in range(NF)
        ]
    )
    lower, upper = ([], [])
    for f in range(NF):
        under = jnp.where(row < 4, rims[f], edge_ref[0, f])
        low = jnp.where(row < 2, pltpu.roll(rims[f], 6, 0), edge_ref[1, f])
        high = jnp.where(row >= 6, pltpu.roll(rims[f], 2, 0), edge_ref[2, f])
        over = jnp.where(row >= 4, rims[f], edge_ref[3, f])
        step = high - low
        lower.append(low + 0.5 * minmod(low - under, step))
        upper.append(high - 0.5 * minmod(step, over - high))
    flux = face_flux(lower, upper, 2)
    rest, parts = (jnp.concatenate(flux, axis=0), [])
    for _ in range(3):
        parts.append(rest.astype(jnp.bfloat16))
        rest = rest - parts[-1].astype(jnp.float32)
    weights = jnp.concatenate(
        [mean_ref[h * LANES : (h + 1) * LANES].astype(jnp.bfloat16) for h in range(2)], axis=1
    )
    stacked = jnp.concatenate(parts, axis=0)
    product = jnp.dot(stacked, weights, preferred_element_type=jnp.float32)
    count = 8 * NF
    product = product[:count] + product[count : 2 * count] + product[2 * count :]
    means = [product[:, h * LANES : (h + 1) * LANES] for h in range(2)]
    tail = 8 * CYCLE - 6 * LANES
    for f in range(NF):
        above = jnp.where(row < 2, pltpu.roll(flux[f], 6, 0), jnp.where(row < 4, 0.0, flux[f]))
        below = jnp.where(row < 4, flux[f], jnp.where(row < 6, 0.0, pltpu.roll(flux[f], 2, 0)))
        change = STEP_RATIO * (below - above)
        for q in range(4):
            at = pl.ds(q * LANES, LANES)
            edges = jnp.where(row == 0, change[q : q + 1], jnp.where(row == 7, change[4 + q : 5 + q], 0.0))
            fine_ref[f, :, at] = fine_in[f, :, at] + edges
        first, last = ([m[f * 8 + r + h : f * 8 + r + h + 1] for h, m in enumerate(means)] for r in (0, 6))
        block_ref[f, :, pl.ds(LANES, 4 * LANES)] = block_in[f, :, pl.ds(LANES, 4 * LANES)]
        block_ref[f, :, pl.ds(0, LANES)] = block_in[f, :, pl.ds(0, LANES)] + STEP_RATIO * (first[0] + first[1])
        turned = lane_roll(jnp.broadcast_to(STEP_RATIO * (last[0] + last[1]), (8, LANES)), 7 * CYCLE)
        at = pl.ds(5 * LANES, LANES)
        block_ref[f, :, at] = block_in[f, :, at] - jnp.where(lane >= 7 * CYCLE - 5 * LANES, turned, 0.0)[0:1]
        at = pl.ds(6 * LANES, tail)
        block_ref[f, :, at] = block_in[f, :, at] - turned[0:1, :tail]


def store_kernel(half, fine_ref, both_ref, fine_hbm, block_hbm, sems):
    partner = jnp.where(lax.axis_index("gx") < half, 1, 0)
    copies = [
        pltpu.make_async_copy(fine_ref, fine_hbm, sems.at[0]),
        pltpu.make_async_copy(both_ref.at[partner], block_hbm, sems.at[1]),
    ]
    for one in copies:
        one.start()
    for one in copies:
        one.wait()


def call(kernel, outs, in_spaces, name, flops, scratch=()):
    single = not isinstance(outs, list)
    shapes = [s if isinstance(s, jax.ShapeDtypeStruct) else pltpu.VMEM(s, jnp.float32) for s in ([outs] if single else outs)]
    specs = [
        pl.BlockSpec(memory_space=pltpu.HBM if isinstance(s, jax.ShapeDtypeStruct) else pltpu.VMEM) for s in shapes
    ]
    return pl.pallas_call(
        kernel,
        out_shape=shapes[0] if single else shapes,
        in_specs=[pl.BlockSpec(memory_space=space) for space in in_spaces],
        out_specs=specs[0] if single else specs,
        scratch_shapes=list(scratch),
        cost_estimate=pl.CostEstimate(flops=flops, bytes_accessed=500_000, transcendentals=0),
        compiler_params=pltpu.CompilerParams(vmem_limit_bytes=16 * 1024 * 1024),
        name=name,
    )


def passed_along(value, axis, steps):
    count = lax.axis_size(axis)
    return lax.ppermute(value, axis, [(source, (source + steps) % count) for source in range(count)])


def local(old_boxes, send_slot, arrival, coarse, coarse_flux):
    V, S, H = (pltpu.VMEM, pltpu.SMEM, pltpu.HBM)
    ghost_m, mean_m, register_m = (jnp.asarray(m) for m in selection_matrices())
    half_axis = lax.axis_size("gx") // 2
    peers = send_slot.shape[2]
    boxes = jnp.transpose(old_boxes[0, 0], (1, 0, 2))
    slots = send_slot[0, 0].T
    block, register = (jnp.transpose(v[0], (1, 0, 2)) for v in (coarse, coarse_flux))
    outgoing, sides = call(
        pack_kernel,
        [(peers, 2 * ROWS, LANES), (NF, 1, FACES_AT + register.shape[2])],
        [H] * 4,
        "pack",
        1_000_000,
        [
            pltpu.SMEM(slots.shape, jnp.int32),
            pltpu.VMEM(boxes.shape, jnp.float32),
            pltpu.VMEM(block.shape, jnp.float32),
            pltpu.VMEM(register.shape, jnp.float32),
            pltpu.SemaphoreType.DMA((4,)),
        ],
    )(*(pltpu.with_memory_space_constraint(v, H) for v in (slots, boxes, block, register)))
    received = lax.all_to_all(outgoing, "gy", split_axis=0, concat_axis=0, tiled=True)
    received = received.reshape(peers * 2 * ROWS, LANES)
    arrive = arrival[0]

    sides = passed_along(sides, "gx", half_axis)
    ghosts, base = call(ghost_kernel, [(NF, 3, 8, LANES), (NF, 8, LANES)], [V] * 3, "ghosts", 10_000_000)(
        sides, ghost_m, register_m
    )
    lowest = lax.dynamic_slice_in_dim(received, arrive[0, 0] * ROWS, ROWS, axis=0)
    highest = lax.dynamic_slice_in_dim(received, arrive[0, 7] * ROWS, ROWS, axis=0)
    before = passed_along(highest, "gy", 1)
    after = passed_along(lowest, "gy", -1)
    fine_shape, block_shape = ((NF, 8, 4 * LANES), (NF, 1, 8 * CYCLE))
    fine, edge, block_new = call(
        side_kernel,
        [fine_shape, (4, NF, 8, LANES), block_shape],
        [S, V, V, V, V],
        "sides",
        50_000_000,
        [pltpu.VMEM((9 * STRIDE, LANES), jnp.float32)],
    )(arrive, received.reshape(peers, 2 * ROWS, LANES), ghosts, base, mean_m)
    fine, block_new = call(
        edge_kernel, [fine_shape, block_shape], [V] * 6, "edges", 20_000_000
    )(before, after, edge, mean_m, fine, block_new)
    pairs = [[g, g + half_axis] for g in range(half_axis)]
    both = lax.all_gather(block_new, "gx", axis_index_groups=pairs)
    fine, back = call(
        functools.partial(store_kernel, half_axis),
        [jax.ShapeDtypeStruct(v, jnp.float32) for v in (fine_shape, block_shape)],
        [V, V],
        "store",
        1_000_000,
        [pltpu.SemaphoreType.DMA((2,))],
    )(fine, pltpu.with_memory_space_constraint(both, V))
    return (jnp.transpose(fine, (1, 0, 2))[None, None], jnp.transpose(back, (1, 0, 2))[None])


def solution(mesh):
    return jax.shard_map(
        local,
        mesh=mesh,
        in_specs=(
            P("gx", "gy", None, None, None),
            P("gx", "gy", None, None),
            P("gx", "gy", None),
            P("gx", "gy", None, None),
            P("gx", "gy", None, None),
        ),
        out_specs=(P("gx", "gy", None, None, None), P("gx", "gy", None, None)),
        check_vma=False,
    )
```

```python
import functools

import jax
import jax.numpy as jnp
import numpy as np
from jax import lax
from jax.experimental import pallas as pl
from jax.experimental.pallas import tpu as pltpu
from jax.sharding import PartitionSpec as P

NF = 5
BXY = 16
EDGE = BXY // 2 + 2
CYCLE = EDGE * EDGE
LANES = 128
STRIDE = 24
FACES_AT = 896
ROWS = 20
STEP_RATIO = 0.1
HIGHEST = lax.Precision.HIGHEST


def lane_iota():
    return lax.broadcasted_iota(jnp.int32, (8, LANES), 1)


def selection_matrices():
    ghost = np.zeros((LANES, 3 * LANES), np.float32)
    mean = np.zeros((5 * LANES, LANES), np.float32)
    for y in range(BXY):
        for x in range(BXY):
            lane = y * BXY + x
            cy, cx = (1 + y // 2, 1 + x // 2)
            mean[lane, cy * EDGE + cx] = 1.0 / 8.0
            if x == 0:
                ghost[cy * EDGE, lane] = 1.0
                mean[2 * LANES + lane, cy * EDGE] = -0.25
            if x == BXY - 1:
                ghost[cy * EDGE + EDGE - 1, lane] = 1.0
                mean[2 * LANES + lane, cy * EDGE + EDGE - 1] = 0.25
            if y == 0:
                ghost[cx, 2 * LANES + x] = 1.0
                mean[4 * LANES + x, cx] = -0.25
            if y == BXY - 1:
                ghost[(EDGE - 1) * EDGE + cx, 2 * LANES + LANES - BXY + x] = 1.0
                mean[4 * LANES + LANES - BXY + x, (EDGE - 1) * EDGE + cx] = 0.25
    register = np.zeros((LANES, LANES), np.float32)
    for t in range(BXY // 2):
        register[t, (1 + t) * EDGE] = 1.0
        register[8 + t, (1 + t) * EDGE + EDGE - 1] = -1.0
        register[16 + t, 1 + t] = 1.0
        register[24 + t, (EDGE - 1) * EDGE + 1 + t] = -1.0
    return (ghost, mean, register)


def minmod(a, b):
    return jnp.maximum(jnp.minimum(a, b), 0.0) + jnp.minimum(jnp.maximum(a, b), 0.0)


def primitive(u):
    inverse = 1.0 / u[0]
    v = [u[i] * inverse for i in (1, 2, 3)]
    pressure = 0.4 * (u[4] - 0.5 * u[0] * (v[0] * v[0] + v[1] * v[1] + v[2] * v[2]))
    return [u[0]] + v + [pressure]


def state_terms(q, normal):
    density, velocity, pressure = (q[0], q[1:4], q[4])
    kinetic = velocity[0] * velocity[0] + velocity[1] * velocity[1] + velocity[2] * velocity[2]
    energy = 2.5 * pressure + 0.5 * density * kinetic
    momentum = [density * v for v in velocity]
    vn = velocity[normal]
    mass = momentum[normal]
    flux = [mass] + [mass * v for v in velocity] + [(energy + pressure) * vn]
    flux[1 + normal] = flux[1 + normal] + pressure
    scaled = 1.4 * pressure
    speed = jnp.abs(vn) + scaled * lax.rsqrt(scaled * density)
    return ([density] + momentum + [energy], flux, speed)


def face_flux(lower, upper, normal):
    cons_l, flux_l, speed_l = state_terms(lower, normal)
    cons_u, flux_u, speed_u = state_terms(upper, normal)
    half = 0.5 * jnp.maximum(speed_l, speed_u)
    return [
        0.5 * (fl + fu) - half * (cu - cl) for fl, fu, cl, cu in zip(flux_l, flux_u, cons_l, cons_u)
    ]


def lane_roll(value, shift):
    return pltpu.roll(value, shift % LANES, 1)


def pack_kernel(slots_hbm, boxes_hbm, coarse_hbm, flux_hbm, out_ref, sides_ref, slots_ref, boxes_ref, coarse_ref, flux_ref, sems):
    cells, faces = (coarse_hbm.shape[2], flux_hbm.shape[2])
    copies = [
        pltpu.make_async_copy(slots_hbm, slots_ref, sems.at[1]),
        pltpu.make_async_copy(boxes_hbm, boxes_ref, sems.at[0]),
        pltpu.make_async_copy(coarse_hbm, coarse_ref, sems.at[2]),
        pltpu.make_async_copy(flux_hbm, flux_ref, sems.at[3]),
    ]
    for one in copies:
        one.start()
    for one in copies[2:]:
        one.wait()
    for f in range(NF):
        sides_ref[f, :, pl.ds(0, cells)] = coarse_ref[f]
        sides_ref[f, :, pl.ds(FACES_AT, faces)] = flux_ref[f]
    for one in copies[:2]:
        one.wait()
    held = boxes_ref.shape[1]
    row = lax.broadcasted_iota(jnp.int32, (8, LANES), 0)

    for d in range(out_ref.shape[0]):
        slots = [jnp.minimum(slots_ref[c, d], held - 1) for c in range(2)]
        lines = [[boxes_ref[f, pl.ds(slot, 1), :] for f in range(NF)] for slot in slots]
        for t in range(2 * ROWS // 8):
            tile = None
            for i in range(8):
                c, r = divmod(8 * t + i, ROWS)
                f, q = divmod(r, 4)
                line = jnp.broadcast_to(lines[c][f][:, q * LANES : (q + 1) * LANES], (8, LANES))
                tile = line if tile is None else jnp.where(row == i, line, tile)
            out_ref[d, 8 * t : 8 * t + 8, :] = tile


def ghost_kernel(sides_ref, ghost_m_ref, register_m_ref, ghosts_ref, base_ref):
    lane = lane_iota()
    row = lax.broadcasted_iota(jnp.int32, (8, LANES), 0)
    on_block = lane < CYCLE
    cy, cx = (lane // EDGE, lane % EDGE)
    interior = (cy >= 1) & (cy <= EDGE - 2) & (cx >= 1) & (cx <= EDGE - 2)
    blocks = []
    registers = []
    for f in range(NF):
        tiles = [sides_ref[f, :, pl.ds(t * LANES, LANES)] for t in range(6)]
        tiles.append(
            jnp.concatenate(
                [sides_ref[f, :, pl.ds(6 * LANES, 8 * CYCLE - 6 * LANES)], jnp.zeros((1, 7 * LANES - 8 * CYCLE), jnp.float32)],
                axis=1,
            )
        )
        rows = []
        for l in range(8):
            start = l * CYCLE
            t, off = divmod(start, LANES)
            first = jnp.broadcast_to(tiles[t], (8, LANES))
            piece = lane_roll(first, -off)
            if off + CYCLE > LANES:
                second = lane_roll(jnp.broadcast_to(tiles[t + 1], (8, LANES)), -off)
                piece = jnp.where(lane < LANES - off, piece, second)
            rows.append(piece)
        block = rows[0]
        for l in range(1, 8):
            block = jnp.where(row == l, rows[l], block)
        blocks.append(block)
        reg = None
        for l in range(8):
            t, off = divmod(l * 32, LANES)
            piece = lane_roll(jnp.broadcast_to(sides_ref[f, :, pl.ds(FACES_AT + t * LANES, LANES)], (8, LANES)), -off)
            reg = piece if reg is None else jnp.where(row == l, piece, reg)
        registers.append(reg)
    safe = [jnp.where(on_block, b, 1.0) for b in blocks]
    prims = jnp.concatenate(primitive(safe), axis=0)
    spread = jnp.dot(prims, ghost_m_ref[...], precision=HIGHEST, preferred_element_type=jnp.float32)
    placed = jnp.dot(
        jnp.concatenate(registers, axis=0), register_m_ref[...], precision=HIGHEST, preferred_element_type=jnp.float32
    )
    for f in range(NF):
        for t in range(3):
            ghosts_ref[f, t] = spread[f * 8 : f * 8 + 8, t * LANES : (t + 1) * LANES]
        kept = jnp.where(on_block & ~interior, blocks[f], 0.0)
        base_ref[f] = kept + (0.5 * STEP_RATIO) * placed[f * 8 : f * 8 + 8]


def side_kernel(arrive_ref, received_ref, ghosts_ref, base_ref, mean_ref, fine_ref, edge_ref, out_ref, boxes):
    for k in range(8):
        source, c = (arrive_ref[0, k] // 2, arrive_ref[0, k] % 2)
        box = jnp.where(c == 0, received_ref[source, :ROWS, :], received_ref[source, ROWS:, :])
        boxes[k * STRIDE : k * STRIDE + ROWS, :] = box
    lane = lane_iota()
    x = lane % BXY
    first_x, last_x = (x == 0, x == BXY - 1)
    low_y, high_y = (lane < BXY, lane >= LANES - BXY)
    cells = [[boxes[pl.ds(f * 4 + q, 8, stride=STRIDE), :] for f in range(NF)] for q in range(4)]
    prims = [primitive(c) for c in cells]
    ghost = [[ghosts_ref[f, t] for f in range(NF)] for t in range(3)]
    change = []
    x_sides = [None, None]
    for q in range(4):
        h = q % 2
        g = ghost[h]
        lower, upper, top = ([], [], [])
        for f in range(NF):
            p = prims[q][f]
            below = jnp.where(first_x, g[f], lane_roll(p, 1))
            above = jnp.where(last_x, g[f], lane_roll(p, -1))
            half = 0.5 * minmod(p - below, above - p)
            high = p + half
            lower.append(jnp.where(first_x, g[f], lane_roll(high, 1)))
            upper.append(p - half)
            top.append((high, jnp.where(last_x, g[f], p)))
        low_flux = face_flux(lower, upper, 0)
        top_flux = face_flux([t[0] for t in top], [t[1] for t in top], 0)
        change.append(
            [jnp.where(last_x, t, lane_roll(l, -1)) - l for l, t in zip(low_flux, top_flux)]
        )
        side = [jnp.where(first_x, l, jnp.where(last_x, t, 0.0)) for l, t in zip(low_flux, top_flux)]
        x_sides[h] = side if x_sides[h] is None else [a + b for a, b in zip(x_sides[h], side)]
    y_sides = None
    for j in range(2):
        q0, q1 = (2 * j, 2 * j + 1)
        g = ghost[2]
        states = ([], [], [], [], [], [])
        for f in range(NF):
            p0, p1 = (prims[q0][f], prims[q1][f])
            up0, up1 = (lane_roll(p0, BXY), lane_roll(p1, BXY))
            down0, down1 = (lane_roll(p0, -BXY), lane_roll(p1, -BXY))
            below0, below1 = (jnp.where(low_y, g[f], up0), jnp.where(low_y, up0, up1))
            above0, above1 = (jnp.where(high_y, down1, down0), jnp.where(high_y, g[f], down1))
            half0 = 0.5 * minmod(p0 - below0, above0 - p0)
            half1 = 0.5 * minmod(p1 - below1, above1 - p1)
            high0, high1 = (p0 + half0, p1 + half1)
            roll0, roll1 = (lane_roll(high0, BXY), lane_roll(high1, BXY))
            for one_list, value in zip(
                states,
                (
                    jnp.where(low_y, g[f], roll0),
                    p0 - half0,
                    jnp.where(low_y, roll0, roll1),
                    p1 - half1,
                    high1,
                    jnp.where(high_y, g[f], p1),
                ),
            ):
                one_list.append(value)
        flux0 = face_flux(states[0], states[1], 1)
        flux1 = face_flux(states[2], states[3], 1)
        top = face_flux(states[4], states[5], 1)
        for f in range(NF):
            next0, next1 = (lane_roll(flux0[f], -BXY), lane_roll(flux1[f], -BXY))
            change[q0][f] = change[q0][f] + (jnp.where(high_y, next1, next0) - flux0[f])
            change[q1][f] = change[q1][f] + (jnp.where(high_y, top[f], next1) - flux1[f])
        side = [jnp.where(low_y, a, jnp.where(high_y, b, 0.0)) for a, b in zip(flux0, top)]
        y_sides = side if y_sides is None else [a + b for a, b in zip(y_sides, side)]
    row = lax.broadcasted_iota(jnp.int32, (8, LANES), 0)
    for h in range(2):
        states = ([], [], [], [])
        for f in range(NF):
            p0, p1 = (prims[h][f], prims[2 + h][f])
            step, under = (p1 - p0, pltpu.roll(p1, 1, 0))
            half0 = 0.5 * minmod(p0 - under, step)
            half1 = 0.5 * minmod(step, pltpu.roll(p0, 7, 0) - p1)
            for one_list, value in zip(
                states, (pltpu.roll(p1 + half1, 1, 0), p0 - half0, p0 + half0, p1 - half1)
            ):
                one_list.append(value)
        flux0 = [jnp.where(row == 0, 0.0, v) for v in face_flux(states[0], states[1], 2)]
        flux1 = [jnp.where((row == 0) | (row == 7), 0.0, v) for v in face_flux(states[2], states[3], 2)]
        for f in range(NF):
            change[h][f] = change[h][f] + (flux1[f] - flux0[f])
            change[2 + h][f] = change[2 + h][f] + (pltpu.roll(flux0[f], 7, 0) - flux1[f])
    parts = [[c - STEP_RATIO * d for c, d in zip(cells[q], change[q])] for q in range(4)]
    for f in range(NF):
        for q in range(4):
            fine_ref[f, :, pl.ds(q * LANES, LANES)] = parts[q][f]
        low, high = ([prims[h][f] for h in range(2)], [prims[2 + h][f] for h in range(2)])
        bottom = {2: [v[0:1] for v in low], 3: [v[0:1] for v in high], 4: [v[1:2] for v in low]}
        top = {0: [v[6:7] for v in high], 1: [v[7:8] for v in low], 2: [v[7:8] for v in high]}
        for place in range(4):
            for face in range(4):
                have, cell = (bottom, place + face) if face < 2 else (top, place + face - 2)
                if cell in have:
                    for h in range(2):
                        edge_ref[place, f, 2 * face + h : 2 * face + h + 1, :] = have[cell][h]
                else:
                    edge_ref[place, f, 2 * face : 2 * face + 2, :] = jnp.zeros((2, LANES), jnp.float32)
    scale = 0.5 * STEP_RATIO
    stacked = jnp.concatenate(
        [
            jnp.concatenate([parts[0][f] + parts[2][f] for f in range(NF)], axis=0),
            jnp.concatenate([parts[1][f] + parts[3][f] for f in range(NF)], axis=0),
            jnp.concatenate([scale * x_sides[0][f] for f in range(NF)], axis=0),
            jnp.concatenate([scale * x_sides[1][f] for f in range(NF)], axis=0),
            jnp.concatenate([scale * y_sides[f] for f in range(NF)], axis=0),
        ],
        axis=1,
    )
    coarse = jnp.dot(stacked, mean_ref[...], precision=HIGHEST, preferred_element_type=jnp.float32)
    cell = row * LANES + lane
    for f in range(NF):
        value = base_ref[f] + coarse[f * 8 : f * 8 + 8]
        for bit in (1, 2, 4):
            value = jnp.where(row & bit != 0, lane_roll(value, bit * CYCLE), value)
        flat = jnp.zeros((8, LANES), jnp.float32)
        for n in range(3):
            shifted = value if n == 0 else pltpu.roll(value, 8 - n, 0)
            flat = jnp.where(cell // CYCLE == row + n, shifted, flat)
        for t in range(6):
            out_ref[f, :, pl.ds(t * LANES, LANES)] = flat[t : t + 1]
        out_ref[f, :, pl.ds(6 * LANES, 8 * CYCLE - 6 * LANES)] = flat[6:7, : 8 * CYCLE - 6 * LANES]


def edge_kernel(before_ref, after_ref, edge_ref, mean_ref, fine_in, block_in, fine_ref, block_ref):
    lane = lane_iota()
    row = lax.broadcasted_iota(jnp.int32, (8, LANES), 0)
    rims = primitive(
        [
            jnp.concatenate([before_ref[f * 4 : f * 4 + 4, :], after_ref[f * 4 : f * 4 + 4, :]], axis=0)
            for f in range(NF)
        ]
    )
    lower, upper = ([], [])
    for f in range(NF):
        under = jnp.where(row < 4, rims[f], edge_ref[0, f])
        low = jnp.where(row < 2, pltpu.roll(rims[f], 6, 0), edge_ref[1, f])
        high = jnp.where(row >= 6, pltpu.roll(rims[f], 2, 0), edge_ref[2, f])
        over = jnp.where(row >= 4, rims[f], edge_ref[3, f])
        step = high - low
        lower.append(low + 0.5 * minmod(low - under, step))
        upper.append(high - 0.5 * minmod(step, over - high))
    flux = face_flux(lower, upper, 2)
    rest, parts = (jnp.concatenate(flux, axis=0), [])
    for _ in range(3):
        parts.append(rest.astype(jnp.bfloat16))
        rest = rest - parts[-1].astype(jnp.float32)
    weights = jnp.concatenate(
        [mean_ref[h * LANES : (h + 1) * LANES].astype(jnp.bfloat16) for h in range(2)], axis=1
    )
    stacked = jnp.concatenate(parts, axis=0)
    product = jnp.dot(stacked, weights, preferred_element_type=jnp.float32)
    count = 8 * NF
    product = product[:count] + product[count : 2 * count] + product[2 * count :]
    means = [product[:, h * LANES : (h + 1) * LANES] for h in range(2)]
    tail = 8 * CYCLE - 6 * LANES
    for f in range(NF):
        above = jnp.where(row < 2, pltpu.roll(flux[f], 6, 0), jnp.where(row < 4, 0.0, flux[f]))
        below = jnp.where(row < 4, flux[f], jnp.where(row < 6, 0.0, pltpu.roll(flux[f], 2, 0)))
        change = STEP_RATIO * (below - above)
        for q in range(4):
            at = pl.ds(q * LANES, LANES)
            edges = jnp.where(row == 0, change[q : q + 1], jnp.where(row == 7, change[4 + q : 5 + q], 0.0))
            fine_ref[f, :, at] = fine_in[f, :, at] + edges
        first, last = ([m[f * 8 + r + h : f * 8 + r + h + 1] for h, m in enumerate(means)] for r in (0, 6))
        block_ref[f, :, pl.ds(LANES, 4 * LANES)] = block_in[f, :, pl.ds(LANES, 4 * LANES)]
        block_ref[f, :, pl.ds(0, LANES)] = block_in[f, :, pl.ds(0, LANES)] + STEP_RATIO * (first[0] + first[1])
        turned = lane_roll(jnp.broadcast_to(STEP_RATIO * (last[0] + last[1]), (8, LANES)), 7 * CYCLE)
        at = pl.ds(5 * LANES, LANES)
        block_ref[f, :, at] = block_in[f, :, at] - jnp.where(lane >= 7 * CYCLE - 5 * LANES, turned, 0.0)[0:1]
        at = pl.ds(6 * LANES, tail)
        block_ref[f, :, at] = block_in[f, :, at] - turned[0:1, :tail]


def store_kernel(half, fine_ref, both_ref, fine_hbm, block_hbm, sems):
    partner = jnp.where(lax.axis_index("gx") < half, 1, 0)
    copies = [
        pltpu.make_async_copy(fine_ref, fine_hbm, sems.at[0]),
        pltpu.make_async_copy(both_ref.at[partner], block_hbm, sems.at[1]),
    ]
    for one in copies:
        one.start()
    for one in copies:
        one.wait()


def call(kernel, outs, in_spaces, name, flops, scratch=()):
    single = not isinstance(outs, list)
    shapes = [s if isinstance(s, jax.ShapeDtypeStruct) else pltpu.VMEM(s, jnp.float32) for s in ([outs] if single else outs)]
    specs = [
        pl.BlockSpec(memory_space=pltpu.HBM if isinstance(s, jax.ShapeDtypeStruct) else pltpu.VMEM) for s in shapes
    ]
    return pl.pallas_call(
        kernel,
        out_shape=shapes[0] if single else shapes,
        in_specs=[pl.BlockSpec(memory_space=space) for space in in_spaces],
        out_specs=specs[0] if single else specs,
        scratch_shapes=list(scratch),
        cost_estimate=pl.CostEstimate(flops=flops, bytes_accessed=500_000, transcendentals=0),
        compiler_params=pltpu.CompilerParams(vmem_limit_bytes=16 * 1024 * 1024),
        name=name,
    )


def passed_along(value, axis, steps):
    count = lax.axis_size(axis)
    return lax.ppermute(value, axis, [(source, (source + steps) % count) for source in range(count)])


def local(old_boxes, send_slot, arrival, coarse, coarse_flux):
    V, S, H = (pltpu.VMEM, pltpu.SMEM, pltpu.HBM)
    ghost_m, mean_m, register_m = (jnp.asarray(m) for m in selection_matrices())
    half_axis = lax.axis_size("gx") // 2
    peers = send_slot.shape[2]
    boxes = jnp.transpose(old_boxes[0, 0], (1, 0, 2))
    slots = send_slot[0, 0].T
    block, register = (jnp.transpose(v[0], (1, 0, 2)) for v in (coarse, coarse_flux))
    outgoing, sides = call(
        pack_kernel,
        [(peers, 2 * ROWS, LANES), (NF, 1, FACES_AT + register.shape[2])],
        [H] * 4,
        "pack",
        1_000_000,
        [
            pltpu.SMEM(slots.shape, jnp.int32),
            pltpu.VMEM(boxes.shape, jnp.float32),
            pltpu.VMEM(block.shape, jnp.float32),
            pltpu.VMEM(register.shape, jnp.float32),
            pltpu.SemaphoreType.DMA((4,)),
        ],
    )(*(pltpu.with_memory_space_constraint(v, H) for v in (slots, boxes, block, register)))
    received = lax.all_to_all(outgoing, "gy", split_axis=0, concat_axis=0, tiled=True)
    received = received.reshape(peers * 2 * ROWS, LANES)
    arrive = arrival[0]

    sides = passed_along(sides, "gx", half_axis)
    ghosts, base = call(ghost_kernel, [(NF, 3, 8, LANES), (NF, 8, LANES)], [V] * 3, "ghosts", 10_000_000)(
        sides, ghost_m, register_m
    )
    lowest = lax.dynamic_slice_in_dim(received, arrive[0, 0] * ROWS, ROWS, axis=0)
    highest = lax.dynamic_slice_in_dim(received, arrive[0, 7] * ROWS, ROWS, axis=0)
    before = passed_along(highest, "gy", 1)
    after = passed_along(lowest, "gy", -1)
    fine_shape, block_shape = ((NF, 8, 4 * LANES), (NF, 1, 8 * CYCLE))
    fine, edge, block_new = call(
        side_kernel,
        [fine_shape, (4, NF, 8, LANES), block_shape],
        [S, V, V, V, V],
        "sides",
        50_000_000,
        [pltpu.VMEM((9 * STRIDE, LANES), jnp.float32)],
    )(arrive, received.reshape(peers, 2 * ROWS, LANES), ghosts, base, mean_m)
    fine, block_new = call(
        edge_kernel, [fine_shape, block_shape], [V] * 6, "edges", 20_000_000
    )(before, after, edge, mean_m, fine, block_new)
    pairs = [[g, g + half_axis] for g in range(half_axis)]
    both = lax.all_gather(block_new, "gx", axis_index_groups=pairs)
    fine, back = call(
        functools.partial(store_kernel, half_axis),
        [jax.ShapeDtypeStruct(v, jnp.float32) for v in (fine_shape, block_shape)],
        [V, V],
        "store",
        1_000_000,
        [pltpu.SemaphoreType.DMA((2,))],
    )(fine, pltpu.with_memory_space_constraint(both, V))
    return (jnp.transpose(fine, (1, 0, 2))[None, None], jnp.transpose(back, (1, 0, 2))[None])


def solution(mesh):
    return jax.shard_map(
        local,
        mesh=mesh,
        in_specs=(
            P("gx", "gy", None, None, None),
            P("gx", "gy", None, None),
            P("gx", "gy", None),
            P("gx", "gy", None, None),
            P("gx", "gy", None, None),
        ),
        out_specs=(P("gx", "gy", None, None, None), P("gx", "gy", None, None)),
        check_vma=False,
    )
```
